256 devices in a mesh: section: 4 (over z_lo, core), seq: 64 (over x, z_hi, y).
Axes of the slice: x: 4, y: 4, z: 8 (z_hi: 4, z_lo: 2; z = z_hi * 2 + z_lo), core: 2. Of those that a mesh axis runs over, the one named last changes fastest.
Arguments:
- stale_out: bfloat16 [4, 2, 4096, 2432], P('section', None, 'seq'), may hold values from -6 to 6
- fresh_latent: bfloat16 [2, 4096, 2432], P(None, 'seq'), may hold values from -6 to 6
- queries: bfloat16 [4, 4096, 4096], P('section', 'seq'), may hold values from -600 to 600
- image_keys: bfloat16 [4, 4096, 4096], P('section', 'seq'), may hold values from -600 to 600
- image_values: bfloat16 [4, 4096, 4096], P('section', 'seq'), may hold values from -6 to 6
- text_keys: bfloat16 [4, 384, 4096], P('section', 'seq'), may hold values from -600 to 600
- text_values: bfloat16 [4, 384, 4096], P('section', 'seq'), may hold values from -12 to 12
- text_count: int32 [2], replicated, may hold values from 1 to 384, as said below
- timesteps: int32 [4, 2], P('section'), may hold values from 0 to 999
- query_gain: float32 [4, 64], P('section'), may hold values from 1 to 2.5
- key_gain: float32 [4, 64], P('section'), may hold values from 1 to 2.5
- out_weight: bfloat16 [4, 2048, 2432], P('section'), may hold values from -0.125 to 0.125
- gate_weight: bfloat16 [4, 256, 2432], P('section', None, 'seq'), may hold values from -0.75 to 0.75
Outputs:
- block_out: bfloat16 [4, 2, 4096, 2432], P('section', None, 'seq')
The draws below stay inside these ranges and needn't reach their ends.
Inputs may be any that keep to these rules, and one draw needn't show every extreme that they name: `text_count`: some image has all 384 slots live.
All inputs are finite; a program needn't handle non-finite values.
Results may differ from the reference program's by a relative error of at most 0.0056.
Values may be sent and summed in bfloat16 or wider, within the bound.
A program may use at most 128 MiB of HBM per device.

```python
import math
import jax
import jax.numpy as jnp
from jax import lax

D = 2432
HD = 64
HEADS = 32
TEMB = 256
NI = 4096
TXT = 384
B = 2
BLOCKS = 4


def scale_rows_cols(base, scale_key, row_count, col_count):
    key_rows, key_cols = jax.random.split(scale_key)
    row_scale = jnp.exp(jax.random.uniform(key_rows, (row_count, 1), jnp.float32, 0.0, math.log(10.0)))
    col_scale = jnp.exp(jax.random.uniform(key_cols, (1, col_count), jnp.float32, 0.0, math.log(10.0)))
    return base * row_scale * col_scale


def projected_draw(key, row_count):
    col_count = B * HEADS * HD
    key_base, key_scale = jax.random.split(key, 2)
    total_rows = BLOCKS * row_count
    base = jnp.clip(jax.random.normal(key_base, (total_rows, col_count), jnp.float32), -6.0, 6.0)
    return scale_rows_cols(base, key_scale, total_rows, col_count).reshape(BLOCKS, row_count, col_count)


def draw_queries(key, part):
    key = jax.random.fold_in(key, 11)
    return projected_draw(key, NI).astype(jnp.bfloat16)


def draw_image_keys(key, part):
    key = jax.random.fold_in(key, 12)
    return projected_draw(key, NI).astype(jnp.bfloat16)


def draw_text_keys(key, part):
    key = jax.random.fold_in(key, 13)
    return projected_draw(key, TXT).astype(jnp.bfloat16)


def draw_text_count(key, part):
    key = jax.random.fold_in(key, 14)
    key_counts, key_full = jax.random.split(key)
    counts = jax.random.randint(key_counts, (B,), 1, TXT + 1)
    full_image = jax.random.randint(key_full, (), 0, B)
    return jnp.where(jnp.arange(B) == full_image, TXT, counts).astype(jnp.int32)


def set_ends(drawn, rng, least, largest):
    place = [jax.random.randint(jax.random.fold_in(rng, axis), (), 0, length) for axis, length in enumerate(drawn.shape)]
    main_axis = drawn.shape.index(max(drawn.shape))
    next_to = place[:main_axis] + [(place[main_axis] + 1) % drawn.shape[main_axis]] + place[main_axis + 1:]
    return drawn.at[tuple(place)].set(least).at[tuple(next_to)].set(largest)


def steps_of(own_key, extent, cuts, smallest, high):
    loudness, own = 1.0, jax.random.fold_in(own_key, 6)
    for axis_at, parts in cuts:
        draws = jnp.exp(jax.random.uniform(jax.random.fold_in(own, axis_at), (parts,), jnp.float32, smallest / len(cuts), high / len(cuts)))
        loudness = loudness * jnp.repeat(draws, extent[axis_at] // parts).reshape([-1 if axis == axis_at else 1 for axis in range(len(extent))])
    return loudness


def normal_values(own_key, extent, spread, most, cuts=(), held_as=jnp.bfloat16):
    array = jax.random.normal(own_key, extent, jnp.float32) * spread
    if len(cuts) > 0:
        array = steps_of(own_key, extent, cuts, -0.22, 0.18) * array
    return jnp.clip(array, min=-most, max=most).astype(held_as)


def setup_inputs(seed: int = 0) -> dict:
    key_of = jax.random.split(jax.random.key(seed), 14)
    return {
        "stale_out": normal_values(key_of[0], (BLOCKS, B, NI, D), 1.0, 6.0, ((0, 4), (2, 64))),
        "fresh_latent": normal_values(key_of[1], (B, NI, D), 1.0, 6.0, ((1, 64),)),
        "queries": draw_queries(jax.random.fold_in(key_of[13], 71), 0),
        "image_keys": draw_image_keys(jax.random.fold_in(key_of[13], 71), 0),
        "image_values": normal_values(key_of[4], (BLOCKS, NI, B * HEADS * HD), 1.0, 6.0, ((0, 4), (1, 64))),
        "text_keys": draw_text_keys(jax.random.fold_in(key_of[13], 71), 0),
        "text_values": normal_values(key_of[6], (BLOCKS, TXT, B * HEADS * HD), 2.0, 12.0, ((0, 4), (1, 64))),
        "text_count": draw_text_count(jax.random.fold_in(key_of[13], 71), 0),
        "timesteps": set_ends(jax.random.randint(key_of[8], (BLOCKS, B), 0, 1000), jax.random.fold_in(key_of[8], 1), 0, 999).astype(jnp.int32),
        "query_gain": jnp.clip(1.0 + 1.5 * jax.random.uniform(key_of[9], (BLOCKS, HD), jnp.float32) ** steps_of(key_of[9], (BLOCKS, HD), ((0, 4),), -0.2, 0.2), 1.0, 2.5),
        "key_gain": jnp.clip(1.0 + 1.5 * jax.random.uniform(key_of[10], (BLOCKS, HD), jnp.float32) ** steps_of(key_of[10], (BLOCKS, HD), ((0, 4),), -0.2, 0.2), 1.0, 2.5),
        "out_weight": normal_values(key_of[11], (BLOCKS, HEADS * HD, D), (HEADS * HD) ** -0.5, 0.125, ((0, 4),)),
        "gate_weight": normal_values(key_of[12], (BLOCKS, TEMB, D), 0.125, 0.75, ((0, 4), (2, 64))),
    }


def head_norm(data, gain):
    row_count = data.shape[0]
    pieces = data.reshape(row_count, -1, gain.shape[-1]).astype(jnp.float32)
    factor = lax.rsqrt(lax.optimization_barrier(jnp.mean(pieces * pieces, axis=-1, keepdims=True)) + 1e-06)
    return (pieces * factor * gain.astype(jnp.float32)).reshape(row_count, -1).astype(jnp.bfloat16)

def attend_item(query_rows, key_rows, value_rows, image_count, text_live):
    query_count, head_size = query_rows.shape
    block_rows = min(512, query_count)
    live_mask = jnp.arange(key_rows.shape[0], dtype=jnp.int32) < image_count + text_live
    blocks = query_rows.reshape(query_count // block_rows, block_rows, head_size)

    def one_block(query_block):
        scores = jnp.einsum('qd,kd->qk', query_block.astype(jnp.float32), key_rows.astype(jnp.float32)) * head_size ** (-0.5)
        weights = jnp.where(live_mask[None, :], jnp.exp(scores), 0.0)
        probs = (weights / lax.optimization_barrier(jnp.sum(weights, axis=1, keepdims=True))).astype(jnp.bfloat16)
        return jnp.einsum('qk,kd->qd', probs.astype(jnp.float32), value_rows.astype(jnp.float32)).astype(jnp.bfloat16)
    return lax.map(one_block, blocks).reshape(query_count, head_size)

def group_attention(query_normed, key_normed, image_vals, text_normed, text_vals, text_count):
    token_count = query_normed.shape[0]
    item_count = query_normed.shape[1] // HD

    def one_item(item_index):
        offset = item_index * HD
        query_rows = lax.dynamic_slice_in_dim(query_normed, offset, HD, 1)
        key_rows = jnp.concatenate([lax.dynamic_slice_in_dim(key_normed, offset, HD, 1), lax.dynamic_slice_in_dim(text_normed, offset, HD, 1)], axis=0)
        value_rows = jnp.concatenate([lax.dynamic_slice_in_dim(image_vals, offset, HD, 1), lax.dynamic_slice_in_dim(text_vals, offset, HD, 1)], axis=0)
        text_live = text_count[item_index // HEADS]
        return attend_item(query_rows, key_rows, value_rows, token_count, text_live)
    results = lax.map(one_item, jnp.arange(item_count, dtype=jnp.int32))
    return jnp.transpose(results, (1, 0, 2)).reshape(token_count, item_count * HD)

def reference(stale_out, fresh_latent, queries, image_keys, image_values, text_keys, text_values, text_count, timesteps, query_gain, key_gain, out_weight, gate_weight):
    block_in = jnp.concatenate([fresh_latent[None], stale_out[:-1]], axis=0)
    half_width = TEMB // 2
    frequency = jnp.exp(-math.log(10000.0) * jnp.arange(half_width, dtype=jnp.float32) / half_width)
    angles = timesteps.astype(jnp.float32)[..., None] * frequency
    features = jnp.concatenate([jnp.cos(angles), jnp.sin(angles)], axis=-1)
    activated = jax.nn.silu(features).astype(jnp.bfloat16)
    gate_vec = jnp.einsum('gbt,gtd->gbd', activated.astype(jnp.float32), gate_weight.astype(jnp.float32))
    results = []
    for group in range(BLOCKS):
        query_normed = head_norm(queries[group], query_gain[group])
        key_normed = head_norm(image_keys[group], key_gain[group])
        text_normed = head_norm(text_keys[group], key_gain[group])
        attended = group_attention(query_normed, key_normed, image_values[group], text_normed, text_values[group], text_count)
        per_image = attended.reshape(NI, B, HEADS * HD)
        projected = jnp.einsum('nbc,cd->bnd', per_image.astype(jnp.float32), out_weight[group].astype(jnp.float32))
        mixed = block_in[group].astype(jnp.float32) + gate_vec[group][:, None, :] * projected
        results.append(mixed.astype(jnp.bfloat16))
    return jnp.stack(results, axis=0)
```

```python
import functools
import math

import jax
import jax.numpy as jnp
from jax import lax
from jax.experimental import pallas as pl
from jax.experimental.pallas import tpu as pltpu
from jax.sharding import PartitionSpec as P

MESH = pl.DeviceIdType.MESH
HD = 64
LANES = 128
TEMB = 256
TEXT_SLOT = 8
SCALE = math.log2(math.e) / math.sqrt(HD)
F32 = jnp.float32
BF16 = jnp.bfloat16


def lanes_below_half(shape):
    return lax.broadcasted_iota(jnp.int32, shape, len(shape) - 1) < HD


def swap_halves(data):
    return pltpu.roll(data, HD, len(data.shape) - 1)


def normed(data, gain):
    squares = data * data
    high = squares.astype(BF16)
    low = (squares - high.astype(F32)).astype(BF16)
    row = lax.broadcasted_iota(jnp.int32, (LANES, LANES), 0) // HD
    col = lax.broadcasted_iota(jnp.int32, (LANES, LANES), 1) // HD
    halves = jnp.where(row == col, 1.0, 0.0).astype(BF16)
    total = jnp.dot(high, halves, preferred_element_type=F32)
    total = total + jnp.dot(low, halves, preferred_element_type=F32)
    return data * lax.rsqrt(total * (1.0 / HD) + 1e-6) * gain


def kernel(
    seq_count,
    group_slots,
    key_tile,
    counts,
    times,
    queries,
    keys,
    values,
    text_keys,
    text_values,
    query_gain,
    key_gain,
    gate_weight,
    out_weight,
    stale,
    fresh,
    out,
    kv_send,
    kv_recv,
    q_send,
    q_recv,
    o_send,
    o_recv,
    text_pad,
    text_k,
    value_aug,
    gate_pad,
    gate_acc,
    weight,
    block_in,
    lhs,
    kv_send_sem,
    kv_recv_sem,
    q_send_sem,
    q_recv_sem,
    o_send_sem,
    o_recv_sem,
    weight_sem,
    shift_send_sem,
    shift_recv_sem,
):
    me = lax.axis_index("seq")
    section = lax.axis_index("section")
    sections = lax.axis_size("section")
    rows = queries.shape[0]
    half = rows // 2
    text_rows = text_keys.shape[0]
    pair_count = seq_count // 2
    gate_span = gate_weight.shape[1]
    groups = seq_count // group_slots
    image_items = seq_count // 2

    barrier = pltpu.get_barrier_semaphore()

    def greet(step, carry):
        pl.semaphore_signal(
            barrier, inc=1, device_id={"seq": lax.rem(me + step, seq_count)}, device_id_type=MESH
        )
        return carry

    lax.fori_loop(1, seq_count, greet, 0)

    @pl.when(section > 0)
    def _():
        pl.semaphore_signal(barrier, inc=1, device_id={"section": section - 1}, device_id_type=MESH)

    load_weight = pltpu.make_async_copy(out_weight, weight, weight_sem)
    load_weight.start()

    text_pad[...] = jnp.zeros_like(text_pad)
    text_pad[0, 0:text_rows, :] = text_keys[...].astype(F32)
    text_pad[1, 0:text_rows, :] = text_values[...].astype(F32)

    row8 = lax.broadcasted_iota(jnp.int32, (8, LANES), 0)
    lane8 = lax.broadcasted_iota(jnp.int32, (8, LANES), 1)
    stamp = jnp.where(row8 % 2 == 0, times[0], times[1]).astype(F32)
    angles = stamp * jnp.exp(lane8.astype(F32) * (-math.log(10000.0) / (TEMB // 2)))
    features = jnp.concatenate([jnp.cos(angles), jnp.sin(angles)], axis=1)
    activated = (features / (1.0 + jnp.exp(-features))).astype(BF16)
    gate_pad[...] = jnp.zeros_like(gate_pad)
    gate_pad[:, 0:gate_span] = jnp.dot(activated, gate_weight[...], preferred_element_type=F32)
    gate_row = pltpu.roll(gate_pad[...], lax.rem(me * gate_span, LANES), 1)
    gate_high = gate_row.astype(BF16).astype(F32)
    gate_low = gate_row - gate_high
    gate_rows = jnp.where(
        row8 < 2,
        gate_high[:, :LANES],
        jnp.where(
            row8 < 4, gate_low[:, :LANES], jnp.where(row8 < 6, gate_high[:, LANES:], gate_low[:, LANES:])
        ),
    )

    @pl.when(section < sections - 1)
    def _():
        pl.semaphore_wait(barrier, seq_count)

    @pl.when(section == sections - 1)
    def _():
        pl.semaphore_wait(barrier, seq_count - 1)

    def send_kv(target, chunk, text_chunk):
        slot = kv_send.at[target]
        slot[0:rows, :] = chunk
        slot[rows:, :] = text_chunk

        @pl.when(target != me)
        def _():
            pltpu.make_async_remote_copy(
                slot, kv_recv.at[me], kv_send_sem, kv_recv_sem, device_id={"seq": target}, device_id_type=MESH
            ).start()

        @pl.when(target == me)
        def _():
            kv_recv[me, 0:rows, :] = chunk
            kv_recv[me, rows:, :] = text_chunk

    def pack_kv(step, carry):
        pair = lax.rem(me // 2 + step, pair_count)
        columns = pl.ds(pl.multiple_of(pair * LANES, LANES), LANES)
        gain = key_gain[...]
        key = normed(keys[:, columns].astype(F32), gain).astype(BF16)
        value = values[:, columns]
        below = lanes_below_half((rows, LANES))
        text_key = normed(text_pad[0, :, columns], gain)
        text_value = text_pad[1, :, columns]
        below8 = lanes_below_half((TEXT_SLOT, LANES))
        first = jnp.where(below, key, swap_halves(value))
        second = jnp.where(below, swap_halves(key), value)
        text_first = jnp.where(below8, text_key, swap_halves(text_value))
        text_second = jnp.where(below8, swap_halves(text_key), text_value)
        send_kv(2 * pair, first, jnp.concatenate([text_first, gate_rows], axis=0).astype(BF16))
        send_kv(2 * pair + 1, second, jnp.concatenate([text_second, gate_rows], axis=0).astype(BF16))
        return carry

    lax.fori_loop(0, pair_count, pack_kv, 0)

    def send_q(target, chunk):
        ahead = lax.rem(target - me + seq_count, seq_count)

        @pl.when(target != me)
        def _():
            q_send[ahead] = chunk
            pltpu.make_async_remote_copy(
                q_send.at[ahead],
                q_recv.at[ahead],
                q_send_sem,
                q_recv_sem.at[ahead // group_slots],
                device_id={"seq": target},
                device_id_type=MESH,
            ).start()

        @pl.when(target == me)
        def _():
            q_recv[0] = chunk

    def pack_q(step, carry):
        pair = lax.rem(me // 2 + step, pair_count)
        columns = pl.ds(pl.multiple_of(pair * LANES, LANES), LANES)
        data = normed(queries[:, columns].astype(F32), query_gain[...]).astype(BF16)
        below = lanes_below_half((half, LANES))
        top, bottom = data[0:half], data[half:]
        send_q(2 * pair, jnp.where(below, top, swap_halves(bottom)))
        send_q(2 * pair + 1, jnp.where(below, swap_halves(top), bottom))
        return carry

    lax.fori_loop(0, pair_count, pack_q, 0)

    @pl.when(section == 0)
    def _():
        pltpu.make_async_copy(fresh, block_in, shift_recv_sem).start()

    shift = pltpu.make_async_remote_copy(
        stale,
        block_in,
        shift_send_sem,
        shift_recv_sem,
        device_id={"section": lax.rem(section + 1, sections)},
        device_id_type=MESH,
    )

    @pl.when(section < sections - 1)
    def _():
        shift.start()

    others = pl.ds(0, seq_count - 1)

    def all_others(send, recv, send_sem, recv_sem):
        return pltpu.make_async_remote_copy(
            send.at[others],
            recv.at[others],
            send_sem,
            recv_sem,
            device_id={"seq": lax.rem(me + 1, seq_count)},
            device_id_type=MESH,
        )

    all_others(kv_send, kv_recv, kv_send_sem, kv_recv_sem).wait_recv()

    live_count = counts[me // image_items]

    def augment(step, carry):
        block = kv_recv[step]
        below = lanes_below_half((rows, LANES))
        value_aug[pl.ds(pl.multiple_of(step * rows, rows), rows), :] = jnp.where(
            below, jnp.ones((), BF16), block[0:rows]
        )
        return carry

    lax.fori_loop(0, seq_count, augment, 0)
    text_total = seq_count * TEXT_SLOT
    image_total = seq_count * rows
    text_all = kv_recv[:, rows : rows + 16, :].astype(F32)[:, 0:TEXT_SLOT, :].reshape(text_total, LANES)
    text_k[...] = text_all.astype(BF16)
    place = lax.broadcasted_iota(jnp.int32, (text_total, LANES), 0)
    within = place % TEXT_SLOT
    live = (within < text_rows) & ((place // TEXT_SLOT) * text_rows + within < live_count)
    value_aug[image_total:, :] = jnp.where(
        live, jnp.where(lanes_below_half((text_total, LANES)), 1.0, text_all), 0.0
    ).astype(BF16)

    gate_acc[...] = jnp.zeros_like(gate_acc)

    def collect_gate(step, carry):
        tile = (step * gate_span) // LANES
        columns = pl.ds(pl.multiple_of(tile * LANES, LANES), LANES)
        gate_acc[:, columns] = gate_acc[:, columns] + kv_recv[step, rows : rows + 16, :].astype(F32)[8:16]
        return carry

    lax.fori_loop(0, seq_count, collect_gate, 0)

    key_blocks = key_tile // rows
    tiles = [(start, key_tile) for start in range(0, image_total, key_tile)]
    tiles += [(image_total + start, min(key_tile, text_total)) for start in range(0, text_total, key_tile)]

    def attend(group, carry):
        first_slot = pl.multiple_of(group * group_slots, group_slots)

        @pl.when(group == 0)
        def _():
            pltpu.make_async_copy(
                q_recv.at[pl.ds(0, group_slots - 1)], q_recv.at[pl.ds(0, group_slots - 1)], q_recv_sem.at[0]
            ).wait()

        @pl.when(group > 0)
        def _():
            pltpu.make_async_copy(
                q_recv.at[pl.ds(0, group_slots)], q_recv.at[pl.ds(0, group_slots)], q_recv_sem.at[group]
            ).wait()

        packed = q_recv[pl.ds(first_slot, group_slots)].reshape(group_slots * half, LANES)
        below = lanes_below_half(packed.shape)
        zero = jnp.zeros((), BF16)
        query = jnp.concatenate(
            [jnp.where(below, packed, zero), jnp.where(below, swap_halves(packed), zero)], axis=0
        )
        total = jnp.zeros((group_slots * rows, LANES), F32)
        for start, size in tiles:
            if start < image_total:
                key = kv_recv[start // rows : (start + size) // rows, 0:rows, :].reshape(size, LANES)
            else:
                key = text_k[start - image_total : start - image_total + size, :]
            scores = lax.dot_general(query, key, (((1,), (1,)), ((), ())), preferred_element_type=F32)
            weights = jnp.exp2(scores * SCALE).astype(BF16)
            total = total + jnp.dot(weights, value_aug[start : start + size, :], preferred_element_type=F32)
        result = total / swap_halves(total)
        top, bottom = result[0 : group_slots * half], result[group_slots * half :]
        mixed = jnp.where(below, swap_halves(top), bottom).astype(BF16)
        o_send[pl.ds(first_slot, group_slots)] = mixed.reshape(group_slots, half, LANES)

        def send_back(step, inner):
            ahead = first_slot + step

            @pl.when(ahead > 0)
            def _():
                pltpu.make_async_remote_copy(
                    o_send.at[ahead],
                    o_recv.at[me],
                    o_send_sem,
                    o_recv_sem,
                    device_id={"seq": lax.rem(me - ahead + seq_count, seq_count)},
                    device_id_type=MESH,
                ).start()

            return inner

        lax.fori_loop(0, group_slots, send_back, 0)
        return carry

    lax.fori_loop(0, groups, attend, 0)
    o_recv[me] = o_send[0]

    load_weight.wait()

    @pl.when(section == 0)
    def _():
        pltpu.make_async_copy(fresh, block_in, shift_recv_sem).wait()

    @pl.when(section > 0)
    def _():
        shift.wait_recv()

    gate_sum = gate_acc[...]
    ahead_tile = gate_sum[4:8, : out.shape[2]]
    gate_first = gate_sum[0:4, : out.shape[2]]
    gate_next = jnp.concatenate([jnp.zeros((4, LANES), F32), ahead_tile[:, : out.shape[2] - LANES]], axis=1)
    gate_four = gate_first + gate_next
    gate_vec = gate_four[0:2] + gate_four[2:4]

    all_others(o_send, o_recv, o_send_sem, o_recv_sem).wait_recv()

    below_half = lanes_below_half((half, LANES))
    for image in range(2):
        for pair in range(image_items // 2):
            one, two = o_recv[image * image_items + 2 * pair], o_recv[image * image_items + 2 * pair + 1]
            columns = slice(pair * LANES, (pair + 1) * LANES)
            lhs[image * rows : image * rows + half, columns] = jnp.where(below_half, one, swap_halves(two))
            lhs[image * rows + half : (image + 1) * rows, columns] = jnp.where(below_half, swap_halves(one), two)

    width = out.shape[2]
    attended = lhs[...]
    for start in range(0, width, 512):
        stop = min(start + 512, width)
        projected = jnp.dot(attended, weight[:, start:stop], preferred_element_type=F32)
        for image in range(2):
            part = projected[image * rows : (image + 1) * rows]
            held = block_in[image, :, start:stop].astype(F32)
            out[image, :, start:stop] = (held + gate_vec[image : image + 1, start:stop] * part).astype(BF16)

    all_others(kv_send, kv_recv, kv_send_sem, kv_recv_sem).wait_send()
    all_others(q_send, q_recv, q_send_sem, q_recv_sem.at[0]).wait_send()
    all_others(o_send, o_recv, o_send_sem, o_recv_sem).wait_send()

    @pl.when(section < sections - 1)
    def _():
        shift.wait_send()


def solution(mesh):
    seq_count = mesh.shape["seq"]
    group_slots = 8
    key_tile = 512

    def step(
        stale,
        fresh,
        queries,
        image_keys,
        image_values,
        text_keys,
        text_values,
        text_count,
        timesteps,
        query_gain,
        key_gain,
        out_weight,
        gate_weight,
    ):
        images, rows, width = fresh.shape
        half = rows // 2
        message = rows + 2 * TEXT_SLOT
        columns = queries.shape[2]
        padded = -(-width // LANES) * LANES + LANES
        vmem = pl.BlockSpec(memory_space=pltpu.VMEM)
        smem = pl.BlockSpec(memory_space=pltpu.SMEM)
        hbm = pl.BlockSpec(memory_space=pl.ANY)
        result = pl.pallas_call(
            functools.partial(kernel, seq_count, group_slots, key_tile),
            out_shape=jax.ShapeDtypeStruct((images, rows, width), BF16),
            in_specs=[smem, smem] + [vmem] * 8 + [hbm] * 3,
            out_specs=vmem,
            scratch_shapes=[
                pltpu.VMEM((seq_count, message, LANES), BF16),
                pltpu.VMEM((seq_count, message, LANES), BF16),
                pltpu.VMEM((seq_count, half, LANES), BF16),
                pltpu.VMEM((seq_count, half, LANES), BF16),
                pltpu.VMEM((seq_count, half, LANES), BF16),
                pltpu.VMEM((seq_count, half, LANES), BF16),
                pltpu.VMEM((2, TEXT_SLOT, columns), F32),
                pltpu.VMEM((seq_count * TEXT_SLOT, LANES), BF16),
                pltpu.VMEM((seq_count * (rows + TEXT_SLOT), LANES), BF16),
                pltpu.VMEM((8, 2 * LANES), F32),
                pltpu.VMEM((8, padded), F32),
                pltpu.VMEM(out_weight.shape[1:], BF16),
                pltpu.VMEM((images, rows, width), BF16),
                pltpu.VMEM((images * rows, out_weight.shape[1]), BF16),
                pltpu.SemaphoreType.DMA,
                pltpu.SemaphoreType.DMA,
                pltpu.SemaphoreType.DMA,
                pltpu.SemaphoreType.DMA((seq_count // group_slots,)),
                pltpu.SemaphoreType.DMA,
                pltpu.SemaphoreType.DMA,
                pltpu.SemaphoreType.DMA,
                pltpu.SemaphoreType.DMA,
                pltpu.SemaphoreType.DMA,
            ],
            compiler_params=pltpu.CompilerParams(
                collective_id=0, has_side_effects=True, vmem_limit_bytes=56 * 1024 * 1024
            ),
            name="joint_attention",
        )(
            text_count,
            timesteps[0],
            queries[0],
            image_keys[0],
            image_values[0],
            text_keys[0],
            text_values[0],
            jnp.tile(query_gain, (1, 2)),
            jnp.tile(key_gain, (1, 2)),
            gate_weight[0],
            out_weight[0],
            stale[0],
            fresh,
        )
        return result[None]

    return jax.shard_map(
        step,
        mesh=mesh,
        in_specs=(
            P("section", None, "seq", None),
            P(None, "seq", None),
            P("section", "seq", None),
            P("section", "seq", None),
            P("section", "seq", None),
            P("section", "seq", None),
            P("section", "seq", None),
            P(),
            P("section", None),
            P("section", None),
            P("section", None),
            P("section", None, None),
            P("section", None, "seq"),
        ),
        out_specs=P("section", None, "seq", None),
        check_vma=False,
    )
```

```python
import functools
import math

import jax
import jax.numpy as jnp
from jax import lax
from jax.experimental import pallas as pl
from jax.experimental.pallas import tpu as pltpu
from jax.sharding import PartitionSpec as P

MESH = pl.DeviceIdType.MESH
HD = 64
LANES = 128
TEMB = 256
TEXT_SLOT = 8
SCALE = math.log2(math.e) / math.sqrt(HD)
F32 = jnp.float32
BF16 = jnp.bfloat16


def lanes_below_half(shape):
    return lax.broadcasted_iota(jnp.int32, shape, len(shape) - 1) < HD


def swap_halves(data):
    return pltpu.roll(data, HD, len(data.shape) - 1)


def normed(parts, gain):
    data = jnp.concatenate(parts, axis=0)
    squares = data * data
    high = squares.astype(BF16)
    low = (squares - high.astype(F32)).astype(BF16)
    row = lax.broadcasted_iota(jnp.int32, (2 * LANES, LANES), 0) // HD
    col = lax.broadcasted_iota(jnp.int32, (2 * LANES, LANES), 1) // HD
    halves = jnp.where(row % 2 == col, 1.0, 0.0).astype(BF16)
    total = jnp.dot(jnp.concatenate([high, low], axis=1), halves, preferred_element_type=F32)
    data = data * lax.rsqrt(total * (1.0 / HD) + 1e-6) * gain
    sizes = [part.shape[0] for part in parts]
    return [data[sum(sizes[:at]) : sum(sizes[: at + 1])] for at in range(len(parts))]


def kernel(
    seq_count,
    span,
    counts,
    times,
    text_keys,
    text_values,
    query_gain,
    key_gain,
    gate_weight,
    queries_hbm,
    keys_hbm,
    values_hbm,
    out_weight,
    stale,
    fresh,
    out,
    queries,
    keys,
    values,
    text_send,
    text_recv,
    q_send,
    q_recv,
    kv_send,
    kv_recv,
    o_send,
    o_recv,
    text_pad,
    text_k,
    text_v,
    value_aug,
    query_rows,
    total,
    gate_pad,
    gate_acc,
    weight,
    block_in,
    projected,
    load_sem,
    text_send_sem,
    text_recv_sem,
    q_send_sem,
    q_recv_sem,
    kv_send_sem,
    kv_recv_sem,
    o_send_sem,
    o_recv_sem,
    shift_send_sem,
    shift_recv_sem,
):
    me = lax.axis_index("seq")
    section = lax.axis_index("section")
    sections = lax.axis_size("section")
    rows = queries.shape[0]
    half = rows // 2
    text_rows = text_keys.shape[0]
    blocks = seq_count // span
    my_block, my_place = me // span, lax.rem(me, span)
    pairs = range(span // 2)
    block_rows = span * rows
    block_columns = span * HD
    gate_span = gate_weight.shape[0]
    width = out.shape[2]
    text_total = seq_count * TEXT_SLOT

    barrier = pltpu.get_barrier_semaphore()

    def greet(step, carry):
        pl.semaphore_signal(
            barrier, inc=1, device_id={"seq": lax.rem(me + step, seq_count)}, device_id_type=MESH
        )
        return carry

    lax.fori_loop(1, seq_count, greet, 0)

    @pl.when(section > 0)
    def _():
        pl.semaphore_signal(barrier, inc=1, device_id={"section": section - 1}, device_id_type=MESH)

    loads = [
        pltpu.make_async_copy(queries_hbm, queries, load_sem.at[0]),
        pltpu.make_async_copy(keys_hbm, keys, load_sem.at[1]),
        pltpu.make_async_copy(values_hbm, values, load_sem.at[2]),
        pltpu.make_async_copy(out_weight, weight, load_sem.at[3]),
    ]
    for load in loads:
        load.start()

    text_pad[...] = jnp.zeros_like(text_pad)
    text_pad[0, 0:text_rows, :] = text_keys[...].astype(F32)
    text_pad[1, 0:text_rows, :] = text_values[...].astype(F32)
    query_gain_both = jnp.concatenate([query_gain[...]] * 2, axis=1)
    key_gain_both = jnp.concatenate([key_gain[...]] * 2, axis=1)

    row8 = lax.broadcasted_iota(jnp.int32, (8, LANES), 0)
    lane8 = lax.broadcasted_iota(jnp.int32, (8, LANES), 1)
    stamp = jnp.where(row8 % 2 == 0, times[0], times[1]).astype(F32)
    angles = stamp * jnp.exp(lane8.astype(F32) * (-math.log(10000.0) / (TEMB // 2)))
    features = jnp.concatenate([jnp.cos(angles), jnp.sin(angles)], axis=1)
    activated = (features / (1.0 + jnp.exp(-features))).astype(BF16)
    gate_pad[...] = jnp.zeros_like(gate_pad)
    gate_pad[:, 0:gate_span] = lax.dot_general(
        activated, gate_weight[...], (((1,), (1,)), ((), ())), preferred_element_type=F32
    )
    gate_row = pltpu.roll(gate_pad[...], lax.rem(me * gate_span, LANES), 1)
    gate_high = gate_row.astype(BF16).astype(F32)
    gate_low = gate_row - gate_high
    gate_rows = jnp.where(
        row8 < 2,
        gate_high[:, :LANES],
        jnp.where(
            row8 < 4, gate_low[:, :LANES], jnp.where(row8 < 6, gate_high[:, LANES:], gate_low[:, LANES:])
        ),
    )

    below = lanes_below_half((rows, LANES))
    below8 = lanes_below_half((TEXT_SLOT, LANES))
    below_half = lanes_below_half((half, LANES))

    def tile(first, at):
        return pl.ds(pl.multiple_of(first * HD + at * LANES, LANES), LANES)

    def push(send, recv, send_sem, recv_sem, target):
        pltpu.make_async_remote_copy(
            send, recv, send_sem, recv_sem, device_id={"seq": target}, device_id_type=MESH
        ).start()

    def pack_text(step, carry):
        first = step * span
        normed_keys = normed([text_pad[0, :, tile(first, at)] for at in pairs], key_gain_both)
        for at, text_key in zip(pairs, normed_keys):
            text_value = text_pad[1, :, tile(first, at)]
            one = jnp.where(below8, text_key, swap_halves(text_value))
            two = jnp.where(below8, swap_halves(text_key), text_value)
            text_send[first + 2 * at] = jnp.concatenate([one, gate_rows], axis=0).astype(BF16)
            text_send[first + 2 * at + 1] = jnp.concatenate([two, gate_rows], axis=0).astype(BF16)
        return carry

    lax.fori_loop(0, blocks, pack_text, 0)
    text_recv[me] = text_send[me]

    @pl.when(section < sections - 1)
    def _():
        pl.semaphore_wait(barrier, seq_count)

    @pl.when(section == sections - 1)
    def _():
        pl.semaphore_wait(barrier, seq_count - 1)

    def send_text(step, carry):
        target = lax.rem(me + step, seq_count)
        push(text_send.at[target], text_recv.at[me], text_send_sem, text_recv_sem, target)
        return carry

    lax.fori_loop(1, seq_count, send_text, 0)

    loads[0].wait()

    def pack_q(step, carry):
        first = lax.rem(my_block + step, blocks) * span
        parts = normed([queries[:, tile(first, at)].astype(F32) for at in pairs], query_gain_both)
        for at, data in zip(pairs, parts):
            data = data.astype(BF16)
            top, bottom = data[0:half], data[half:]
            q_send[first + 2 * at] = jnp.where(below_half, top, swap_halves(bottom))
            q_send[first + 2 * at + 1] = jnp.where(below_half, swap_halves(top), bottom)
        for turn in range(span):
            target = first + lax.rem(my_place + turn, span)
            slot = step * span + turn

            @pl.when(slot > 0)
            def _(target=target, slot=slot):
                push(q_send.at[target], q_recv.at[slot], q_send_sem, q_recv_sem, target)

        return carry

    lax.fori_loop(0, blocks, pack_q, 0)
    q_recv[0] = q_send[me]

    loads[1].wait()
    loads[2].wait()

    def pack_kv(step, carry):
        first = lax.rem(my_block + step, blocks) * span
        parts = normed([keys[:, tile(first, at)].astype(F32) for at in pairs], key_gain_both)
        for at, key in zip(pairs, parts):
            key = key.astype(BF16)
            value = values[:, tile(first, at)]
            kv_send[first + 2 * at] = jnp.where(below, key, swap_halves(value))
            kv_send[first + 2 * at + 1] = jnp.where(below, swap_halves(key), value)
        for turn in range(span):
            target = first + lax.rem(my_place + turn, span)
            slot = step * span + turn

            @pl.when(slot > 0)
            def _(target=target, slot=slot):
                push(kv_send.at[target], kv_recv.at[slot], kv_send_sem, kv_recv_sem.at[step], target)

        return carry

    lax.fori_loop(0, blocks, pack_kv, 0)
    kv_recv[0] = kv_send[me]

    @pl.when(section == 0)
    def _():
        pltpu.make_async_copy(fresh, block_in, shift_recv_sem).start()

    shift = pltpu.make_async_remote_copy(
        stale,
        block_in,
        shift_send_sem,
        shift_recv_sem,
        device_id={"section": lax.rem(section + 1, sections)},
        device_id_type=MESH,
    )

    @pl.when(section < sections - 1)
    def _():
        shift.start()

    def await_slots(recv, count, sem):
        part = recv.at[pl.ds(0, count)]
        pltpu.make_async_copy(part, part, sem).wait()

    def await_step(recv, step, sem):
        @pl.when(step == 0)
        def _():
            await_slots(recv, span - 1, sem.at[0])

        @pl.when(step > 0)
        def _():
            await_slots(recv, span, sem.at[step])

    await_slots(text_recv, seq_count - 1, text_recv_sem)
    live_count = counts[me // (seq_count // 2)]
    text_all = text_recv[...].astype(F32)[:, 0:TEXT_SLOT, :].reshape(text_total, LANES)
    text_k[...] = text_all.astype(BF16)
    place = lax.broadcasted_iota(jnp.int32, (text_total, LANES), 0)
    within = place % TEXT_SLOT
    live = (within < text_rows) & ((place // TEXT_SLOT) * text_rows + within < live_count)
    text_v[...] = jnp.where(
        live, jnp.where(lanes_below_half((text_total, LANES)), 1.0, text_all), 0.0
    ).astype(BF16)
    gate_acc[...] = jnp.zeros_like(gate_acc)

    def collect_gate(step, carry):
        at = (step * gate_span) // LANES
        columns = pl.ds(pl.multiple_of(at * LANES, LANES), LANES)
        gate_acc[:, columns] = gate_acc[:, columns] + text_recv[step].astype(F32)[TEXT_SLOT:]
        return carry

    lax.fori_loop(0, seq_count, collect_gate, 0)

    await_slots(q_recv, seq_count - 1, q_recv_sem)
    left = lanes_below_half((block_rows // 2, LANES))

    def rows_of(block):
        return pl.ds(pl.multiple_of(block * block_rows, block_rows), block_rows)

    def spread(block, carry):
        packed = q_recv[pl.ds(pl.multiple_of(block * span, span), span)].reshape(block_rows // 2, LANES)
        zero = jnp.zeros((), BF16)
        query_rows[rows_of(block), :] = jnp.concatenate(
            [jnp.where(left, packed, zero), jnp.where(left, swap_halves(packed), zero)], axis=0
        )
        return carry

    lax.fori_loop(0, blocks, spread, 0)

    def attend(block, key, value):
        scores = lax.dot_general(
            query_rows[rows_of(block), :], key, (((1,), (1,)), ((), ())), preferred_element_type=F32
        )
        weights = jnp.exp2(scores * SCALE).astype(BF16)
        return jnp.dot(weights, value, preferred_element_type=F32)

    def attend_text(block, carry):
        total[rows_of(block), :] = attend(block, text_k[...], text_v[...])
        return carry

    lax.fori_loop(0, blocks, attend_text, 0)

    def keys_of(step):
        return kv_recv[pl.ds(pl.multiple_of(step * span, span), span)].reshape(block_rows, LANES)

    def prepare(step):
        await_step(kv_recv, step, kv_recv_sem)
        value_aug[...] = jnp.where(lanes_below_half((block_rows, LANES)), jnp.ones((), BF16), keys_of(step))

    def attend_step(step, carry):
        prepare(step)

        def attend_block(block, inner):
            total[rows_of(block), :] += attend(block, keys_of(step), value_aug[...])
            return inner

        lax.fori_loop(0, blocks, attend_block, 0)
        return carry

    lax.fori_loop(0, blocks - 1, attend_step, 0)

    prepare(blocks - 1)

    def finish_block(block, carry):
        summed = total[rows_of(block), :] + attend(block, keys_of(blocks - 1), value_aug[...])
        result = summed / swap_halves(summed)
        top, bottom = result[0 : block_rows // 2], result[block_rows // 2 :]
        mixed = jnp.where(left, swap_halves(top), bottom).astype(BF16)
        o_send[pl.ds(pl.multiple_of(block * span, span), span)] = mixed.reshape(span, half, LANES)
        first = lax.rem(my_block - block + blocks, blocks) * span
        for turn in range(span):
            source = first + lax.rem(my_place - turn + span, span)
            slot = block * span + turn

            @pl.when(slot > 0)
            def _(source=source, slot=slot):
                push(o_send.at[slot], o_recv.at[me], o_send_sem, o_recv_sem.at[block], source)

        return carry

    lax.fori_loop(0, blocks, finish_block, 0)
    o_recv[me] = o_send[0]

    loads[3].wait()
    projected[...] = jnp.zeros_like(projected)

    def project(step, carry):
        await_step(o_recv, step, o_recv_sem)
        block = lax.rem(my_block + step, blocks)
        image = block // (blocks // 2)
        weight_rows = pl.ds(
            pl.multiple_of(lax.rem(block, blocks // 2) * block_columns, block_columns), block_columns
        )
        tops, bottoms = [], []
        for at in pairs:
            one, two = o_recv[block * span + 2 * at], o_recv[block * span + 2 * at + 1]
            tops.append(jnp.where(below_half, one, swap_halves(two)))
            bottoms.append(jnp.where(below_half, swap_halves(one), two))
        attended = jnp.concatenate(
            [jnp.concatenate(tops, axis=1), jnp.concatenate(bottoms, axis=1)], axis=0
        )
        for start in range(0, width, 512):
            stop = min(start + 512, width)
            projected[image, :, start:stop] += jnp.dot(
                attended, weight[weight_rows, start:stop], preferred_element_type=F32
            )
        return carry

    lax.fori_loop(0, blocks, project, 0)

    @pl.when(section == 0)
    def _():
        pltpu.make_async_copy(fresh, block_in, shift_recv_sem).wait()

    @pl.when(section > 0)
    def _():
        shift.wait_recv()

    gate_sum = gate_acc[...]
    gate_next = jnp.concatenate([jnp.zeros((4, LANES), F32), gate_sum[4:8, : width - LANES]], axis=1)
    gate_four = gate_sum[0:4, :width] + gate_next
    gate_vec = gate_four[0:2] + gate_four[2:4]
    for image in range(2):
        held = block_in[image].astype(F32)
        out[image] = (held + gate_vec[image : image + 1] * projected[image]).astype(BF16)

    for send, sem in (
        (text_send, text_send_sem),
        (q_send, q_send_sem),
        (kv_send, kv_send_sem),
        (o_send, o_send_sem),
    ):
        await_slots(send, seq_count - 1, sem)

    @pl.when(section < sections - 1)
    def _():
        shift.wait_send()


def solution(mesh):
    seq_count = mesh.shape["seq"]
    span = 8

    def step(
        stale,
        fresh,
        queries,
        image_keys,
        image_values,
        text_keys,
        text_values,
        text_count,
        timesteps,
        query_gain,
        key_gain,
        out_weight,
        gate_weight,
    ):
        images, rows, width = fresh.shape
        half = rows // 2
        columns = queries.shape[2]
        padded = -(-width // LANES) * LANES + LANES
        blocks = seq_count // span
        vmem = pl.BlockSpec(memory_space=pltpu.VMEM)
        smem = pl.BlockSpec(memory_space=pltpu.SMEM)
        hbm = pl.BlockSpec(memory_space=pl.ANY)
        dma = pltpu.SemaphoreType.DMA
        text_total = seq_count * TEXT_SLOT
        result = pl.pallas_call(
            functools.partial(kernel, seq_count, span),
            out_shape=jax.ShapeDtypeStruct((images, rows, width), BF16),
            in_specs=[smem, smem] + [vmem] * 5 + [hbm] * 6,
            out_specs=vmem,
            scratch_shapes=[
                pltpu.VMEM((rows, columns), BF16),
                pltpu.VMEM((rows, columns), BF16),
                pltpu.VMEM((rows, columns), BF16),
                pltpu.VMEM((seq_count, 2 * TEXT_SLOT, LANES), BF16),
                pltpu.VMEM((seq_count, 2 * TEXT_SLOT, LANES), BF16),
                pltpu.VMEM((seq_count, half, LANES), BF16),
                pltpu.VMEM((seq_count, half, LANES), BF16),
                pltpu.VMEM((seq_count, rows, LANES), BF16),
                pltpu.VMEM((seq_count, rows, LANES), BF16),
                pltpu.VMEM((seq_count, half, LANES), BF16),
                pltpu.VMEM((seq_count, half, LANES), BF16),
                pltpu.VMEM((2, TEXT_SLOT, columns), F32),
                pltpu.VMEM((text_total, LANES), BF16),
                pltpu.VMEM((text_total, LANES), BF16),
                pltpu.VMEM((span * rows, LANES), BF16),
                pltpu.VMEM((seq_count * rows, LANES), BF16),
                pltpu.VMEM((seq_count * rows, LANES), F32),
                pltpu.VMEM((8, 2 * LANES), F32),
                pltpu.VMEM((8, padded), F32),
                pltpu.VMEM(out_weight.shape[1:], BF16),
                pltpu.VMEM((images, rows, width), BF16),
                pltpu.VMEM((images, rows, width), F32),
                dma((4,)),
                dma,
                dma,
                dma,
                dma,
                dma,
                dma((blocks,)),
                dma,
                dma((blocks,)),
                dma,
                dma,
            ],
            compiler_params=pltpu.CompilerParams(
                collective_id=0, has_side_effects=True, vmem_limit_bytes=56 * 1024 * 1024
            ),
            name="joint_attention",
        )(
            text_count,
            timesteps[0],
            text_keys[0],
            text_values[0],
            query_gain,
            key_gain,
            gate_weight[0].T,
            queries[0],
            image_keys[0],
            image_values[0],
            out_weight[0],
            stale[0],
            fresh,
        )
        return result[None]

    return jax.shard_map(
        step,
        mesh=mesh,
        in_specs=(
            P("section", None, "seq", None),
            P(None, "seq", None),
            P("section", "seq", None),
            P("section", "seq", None),
            P("section", "seq", None),
            P("section", "seq", None),
            P("section", "seq", None),
            P(),
            P("section", None),
            P("section", None),
            P("section", None),
            P("section", None, None),
            P("section", None, "seq"),
        ),
        out_specs=P("section", None, "seq", None),
        check_vma=False,
    )
```

```python
import functools
import math

import jax
import jax.numpy as jnp
from jax import lax
from jax.experimental import pallas as pl
from jax.experimental.pallas import tpu as pltpu
from jax.sharding import PartitionSpec as P

MESH = pl.DeviceIdType.MESH
HD = 64
LANES = 128
TEMB = 256
TEXT_SLOT = 8
SCALE = math.log2(math.e) / math.sqrt(HD)
F32 = jnp.float32
BF16 = jnp.bfloat16


def lanes_below_half(shape):
    return lax.broadcasted_iota(jnp.int32, shape, len(shape) - 1) < HD


def swap_halves(data):
    return pltpu.roll(data, HD, len(data.shape) - 1)


def normed(parts, gain):
    data = jnp.concatenate(parts, axis=0)
    squares = data * data
    high = squares.astype(BF16)
    low = (squares - high.astype(F32)).astype(BF16)
    row = lax.broadcasted_iota(jnp.int32, (2 * LANES, LANES), 0) // HD
    col = lax.broadcasted_iota(jnp.int32, (2 * LANES, LANES), 1) // HD
    halves = jnp.where(row % 2 == col, 1.0, 0.0).astype(BF16)
    total = jnp.dot(jnp.concatenate([high, low], axis=1), halves, preferred_element_type=F32)
    data = data * lax.rsqrt(total * (1.0 / HD) + 1e-6) * gain
    sizes = [part.shape[0] for part in parts]
    return [data[sum(sizes[:at]) : sum(sizes[: at + 1])] for at in range(len(parts))]


def kernel(
    seq_count,
    span,
    early,
    counts,
    times,
    text_keys,
    text_values,
    query_gain,
    key_gain,
    gate_weight,
    queries_hbm,
    keys_hbm,
    values_hbm,
    out_weight,
    stale,
    fresh,
    out,
    queries,
    keys,
    values,
    text_send,
    text_recv,
    q_send,
    q_recv,
    kv_send,
    kv_recv,
    o_send,
    o_recv,
    text_pad,
    text_k,
    text_v,
    value_aug,
    query_rows,
    total,
    gate_pad,
    gate_acc,
    weight,
    block_in,
    projected,
    load_sem,
    text_send_sem,
    text_recv_sem,
    q_send_sem,
    q_recv_sem,
    kv_send_sem,
    kv_recv_sem,
    o_send_sem,
    o_recv_sem,
    shift_send_sem,
    shift_recv_sem,
):
    me = lax.axis_index("seq")
    section = lax.axis_index("section")
    sections = lax.axis_size("section")
    rows = queries.shape[0]
    half = rows // 2
    text_rows = text_keys.shape[0]
    blocks = seq_count // span
    my_block = (me // 16) * 2 + (me % 4) // 2
    my_place = ((me // 4) % 4) * 2 + me % 2
    my_label = my_block * span + my_place

    def device_at(block, place):
        return (block // 2) * 16 + (place // 2) * 4 + (block % 2) * 2 + place % 2

    def tile_index(block, at):
        return (block // 2) * 8 + at * 2 + block % 2

    pairs = range(span // 2)
    block_rows = span * rows
    gate_span = gate_weight.shape[0]
    width = out.shape[2]
    text_total = seq_count * TEXT_SLOT

    barrier = pltpu.get_barrier_semaphore()

    def greet(step, carry):
        pl.semaphore_signal(
            barrier, inc=1, device_id={"seq": lax.rem(me + step, seq_count)}, device_id_type=MESH
        )
        return carry

    lax.fori_loop(1, seq_count, greet, 0)

    @pl.when(section > 0)
    def _():
        pl.semaphore_signal(barrier, inc=1, device_id={"section": section - 1}, device_id_type=MESH)

    loads = [
        pltpu.make_async_copy(queries_hbm, queries, load_sem.at[0]),
        pltpu.make_async_copy(keys_hbm, keys, load_sem.at[1]),
        pltpu.make_async_copy(values_hbm, values, load_sem.at[2]),
        pltpu.make_async_copy(out_weight, weight, load_sem.at[3]),
    ]
    for load in loads:
        load.start()

    text_pad[...] = jnp.zeros_like(text_pad)
    text_pad[0, 0:text_rows, :] = text_keys[...].astype(F32)
    text_pad[1, 0:text_rows, :] = text_values[...].astype(F32)
    query_gain_both = jnp.concatenate([query_gain[...]] * 2, axis=1)
    key_gain_both = jnp.concatenate([key_gain[...]] * 2, axis=1)

    row8 = lax.broadcasted_iota(jnp.int32, (8, LANES), 0)
    lane8 = lax.broadcasted_iota(jnp.int32, (8, LANES), 1)
    stamp = jnp.where(row8 % 2 == 0, times[0], times[1]).astype(F32)
    angles = stamp * jnp.exp(lane8.astype(F32) * (-math.log(10000.0) / (TEMB // 2)))
    features = jnp.concatenate([jnp.cos(angles), jnp.sin(angles)], axis=1)
    activated = (features / (1.0 + jnp.exp(-features))).astype(BF16)
    gate_pad[...] = jnp.zeros_like(gate_pad)
    gate_pad[:, 0:gate_span] = lax.dot_general(
        activated, gate_weight[...], (((1,), (1,)), ((), ())), preferred_element_type=F32
    )
    gate_share = gate_pad[...]
    gate_high = gate_share.astype(BF16).astype(F32)
    gate_rows = jnp.where(lane8 < HD, gate_high, swap_halves(gate_share - gate_high))

    below = lanes_below_half((rows, LANES))
    below8 = lanes_below_half((TEXT_SLOT, LANES))
    below_half = lanes_below_half((half, LANES))

    def tile(index):
        return pl.ds(pl.multiple_of(index * LANES, LANES), LANES)

    def push(send, recv, send_sem, recv_sem, target):
        pltpu.make_async_remote_copy(
            send, recv, send_sem, recv_sem, device_id={"seq": target}, device_id_type=MESH
        ).start()

    def pack_text(step, carry):
        first = step * span
        normed_keys = normed([text_pad[0, :, tile(first // 2 + at)] for at in pairs], key_gain_both)
        for at, text_key in zip(pairs, normed_keys):
            text_value = text_pad[1, :, tile(first // 2 + at)]
            one = jnp.where(below8, text_key, swap_halves(text_value))
            two = jnp.where(below8, swap_halves(text_key), text_value)
            text_send[first + 2 * at] = jnp.where(row8 < text_rows, one, gate_rows).astype(BF16)
            text_send[first + 2 * at + 1] = jnp.where(row8 < text_rows, two, gate_rows).astype(BF16)
        return carry

    lax.fori_loop(0, blocks, pack_text, 0)
    text_recv[me] = text_send[me]

    @pl.when(section < sections - 1)
    def _():
        pl.semaphore_wait(barrier, seq_count)

    @pl.when(section == sections - 1)
    def _():
        pl.semaphore_wait(barrier, seq_count - 1)

    def send_text(step, carry):
        target = lax.rem(me + step, seq_count)
        push(text_send.at[target], text_recv.at[me], text_send_sem, text_recv_sem, target)
        return carry

    lax.fori_loop(1, seq_count, send_text, 0)

    loads[0].wait()

    def pack_q(step, carry):
        block = lax.rem(my_block + step, blocks)
        first = block * span
        parts = normed([queries[:, tile(tile_index(block, at))].astype(F32) for at in pairs], query_gain_both)
        for at, data in zip(pairs, parts):
            data = data.astype(BF16)
            top, bottom = data[0:half], data[half:]
            q_send[first + 2 * at] = jnp.where(below_half, top, swap_halves(bottom))
            q_send[first + 2 * at + 1] = jnp.where(below_half, swap_halves(top), bottom)
        for turn in range(span):
            place = lax.rem(my_place + turn, span)
            slot = step * span + turn

            @pl.when(slot > 0)
            def _(place=place, slot=slot):
                push(
                    q_send.at[first + place],
                    q_recv.at[slot],
                    q_send_sem,
                    q_recv_sem.at[step],
                    device_at(block, place),
                )

        return carry

    lax.fori_loop(0, early, pack_q, 0)
    q_recv[0] = q_send[my_label]

    loads[1].wait()
    loads[2].wait()

    def pack_kv(step, carry):
        block = lax.rem(my_block + step, blocks)
        first = block * span
        parts = normed([keys[:, tile(tile_index(block, at))].astype(F32) for at in pairs], key_gain_both)
        for at, key in zip(pairs, parts):
            key = key.astype(BF16)
            value = values[:, tile(tile_index(block, at))]
            kv_send[first + 2 * at] = jnp.where(below, key, swap_halves(value))
            kv_send[first + 2 * at + 1] = jnp.where(below, swap_halves(key), value)
        for turn in range(span):
            place = lax.rem(my_place + turn, span)
            slot = step * span + turn

            @pl.when(slot > 0)
            def _(place=place, slot=slot):
                push(
                    kv_send.at[first + place],
                    kv_recv.at[slot],
                    kv_send_sem,
                    kv_recv_sem.at[step],
                    device_at(block, place),
                )

        return carry

    lax.fori_loop(0, blocks, pack_kv, 0)
    kv_recv[0] = kv_send[my_label]

    lax.fori_loop(early, blocks, pack_q, 0)

    @pl.when(section == 0)
    def _():
        pltpu.make_async_copy(fresh, block_in, shift_recv_sem).start()

    shift = pltpu.make_async_remote_copy(
        stale,
        block_in,
        shift_send_sem,
        shift_recv_sem,
        device_id={"section": lax.rem(section + 1, sections)},
        device_id_type=MESH,
    )

    @pl.when(section < sections - 1)
    def _():
        shift.start()

    def await_slots(recv, count, sem):
        part = recv.at[pl.ds(0, count)]
        pltpu.make_async_copy(part, part, sem).wait()

    def await_step(recv, step, sem):
        if isinstance(step, int):
            await_slots(recv, span if step else span - 1, sem.at[step])
            return

        @pl.when(step == 0)
        def _():
            await_slots(recv, span - 1, sem.at[0])

        @pl.when(step > 0)
        def _():
            await_slots(recv, span, sem.at[step])

    await_slots(text_recv, seq_count - 1, text_recv_sem)
    live_count = counts[me // (seq_count // 2)]
    text_all = text_recv[...].astype(F32).reshape(text_total, LANES)
    place = lax.broadcasted_iota(jnp.int32, (text_total, LANES), 0)
    within = place % TEXT_SLOT
    text_k[...] = jnp.where(within < text_rows, text_all, 0.0).astype(BF16)
    live = (within < text_rows) & ((place // TEXT_SLOT) * text_rows + within < live_count)
    text_v[...] = jnp.where(
        live, jnp.where(lanes_below_half((text_total, LANES)), 1.0, text_all), 0.0
    ).astype(BF16)
    gate_tiles = [jnp.zeros((TEXT_SLOT, LANES), F32) for _ in range(width // LANES)]
    for source in range(seq_count):
        at, ahead = divmod(source * gate_span, LANES)
        share = text_recv[source].astype(F32)
        share = jnp.where(below8, share + swap_halves(share), 0.0)
        if ahead > 0:
            share = pltpu.roll(share, ahead, 1)
        if ahead + gate_span > LANES:
            gate_tiles[at + 1] = gate_tiles[at + 1] + jnp.where(lane8 < ahead, share, 0.0)
            share = jnp.where(lane8 < ahead, 0.0, share)
        gate_tiles[at] = gate_tiles[at] + share
    for at, gate_tile in enumerate(gate_tiles):
        gate_acc[:, at * LANES : (at + 1) * LANES] = gate_tile

    left = lanes_below_half((block_rows // 2, LANES))

    def rows_of(block):
        start = block * block_rows
        return pl.ds(start if isinstance(start, int) else pl.multiple_of(start, block_rows), block_rows)

    def slots_of(block):
        start = block * span
        return pl.ds(start if isinstance(start, int) else pl.multiple_of(start, span), span)

    def spread(block):
        await_step(q_recv, block, q_recv_sem)
        packed = q_recv[slots_of(block)].reshape(block_rows // 2, LANES)
        zero = jnp.zeros((), BF16)
        query_rows[rows_of(block), :] = jnp.concatenate(
            [jnp.where(left, packed, zero), jnp.where(left, swap_halves(packed), zero)], axis=0
        )

    def attend(block, key, value):
        scores = lax.dot_general(
            query_rows[rows_of(block), :], key, (((1,), (1,)), ((), ())), preferred_element_type=F32
        )
        weights = jnp.exp2(scores * SCALE).astype(BF16)
        return jnp.dot(weights, value, preferred_element_type=F32)

    def keys_of(step):
        return kv_recv[slots_of(step)].reshape(block_rows, LANES)

    def prepare(step):
        await_step(kv_recv, step, kv_recv_sem)
        value_aug[rows_of(step), :] = jnp.where(
            lanes_below_half((block_rows, LANES)), jnp.ones((), BF16), keys_of(step)
        )

    def attend_step(block, step):
        return attend(block, keys_of(step), value_aug[rows_of(step), :])

    def finish(block, summed):
        result = summed / swap_halves(summed)
        top, bottom = result[0 : block_rows // 2], result[block_rows // 2 :]
        mixed = jnp.where(left, swap_halves(top), bottom).astype(BF16)
        o_send[slots_of(block)] = mixed.reshape(span, half, LANES)
        from_block = lax.rem(my_block - block + blocks, blocks)
        for turn in range(span):
            source = device_at(from_block, lax.rem(my_place - turn + span, span))
            slot = block * span + turn
            if not isinstance(slot, int) or slot > 0:
                push(o_send.at[slot], o_recv.at[my_label], o_send_sem, o_recv_sem.at[block], source)

    for block in range(early):
        spread(block)
    for block in range(early):
        total[rows_of(block), :] = attend(block, text_k[...], text_v[...])

    def meet(step, carry):
        prepare(step)
        for block in range(early):
            total[rows_of(block), :] += attend_step(block, step)
        return carry

    lax.fori_loop(0, blocks - 1, meet, 0)
    prepare(blocks - 1)
    for block in range(early):
        finish(block, total[rows_of(block), :] + attend_step(block, blocks - 1))

    def attend_all(block, carry):
        spread(block)
        summed = attend(block, text_k[...], text_v[...])
        for step in range(blocks):
            summed = summed + attend_step(block, step)
        finish(block, summed)
        return carry

    lax.fori_loop(early, blocks, attend_all, 0)
    o_recv[my_label] = o_send[0]

    loads[3].wait()
    projected[...] = jnp.zeros_like(projected)

    def project(step, carry):
        await_step(o_recv, step, o_recv_sem)
        block = lax.rem(my_block + step, blocks)
        image = block // (blocks // 2)
        weight_tiles = [tile(lax.rem(tile_index(block, at), seq_count // 4)) for at in pairs]
        tops, bottoms = [], []
        for at in pairs:
            one, two = o_recv[block * span + 2 * at], o_recv[block * span + 2 * at + 1]
            tops.append(jnp.where(below_half, one, swap_halves(two)))
            bottoms.append(jnp.where(below_half, swap_halves(one), two))
        attended = jnp.concatenate(
            [jnp.concatenate(tops, axis=1), jnp.concatenate(bottoms, axis=1)], axis=0
        )
        for start in range(0, width, 512):
            stop = min(start + 512, width)
            part = jnp.concatenate([weight[part_rows, start:stop] for part_rows in weight_tiles], axis=0)
            projected[image, :, start:stop] += jnp.dot(attended, part, preferred_element_type=F32)
        return carry

    lax.fori_loop(0, blocks, project, 0)

    @pl.when(section == 0)
    def _():
        pltpu.make_async_copy(fresh, block_in, shift_recv_sem).wait()

    @pl.when(section > 0)
    def _():
        shift.wait_recv()

    gate_vec = gate_acc[text_rows : text_rows + 2, :]
    for image in range(2):
        held = block_in[image].astype(F32)
        out[image] = (held + gate_vec[image : image + 1] * projected[image]).astype(BF16)

    for send, sem in (
        (text_send, text_send_sem),
        (q_send, q_send_sem),
        (kv_send, kv_send_sem),
        (o_send, o_send_sem),
    ):
        await_slots(send, seq_count - 1, sem)

    @pl.when(section < sections - 1)
    def _():
        shift.wait_send()


def solution(mesh):
    seq_count = mesh.shape["seq"]
    span = 8
    early = 6

    def step(
        stale,
        fresh,
        queries,
        image_keys,
        image_values,
        text_keys,
        text_values,
        text_count,
        timesteps,
        query_gain,
        key_gain,
        out_weight,
        gate_weight,
    ):
        images, rows, width = fresh.shape
        half = rows // 2
        columns = queries.shape[2]
        blocks = seq_count // span
        vmem = pl.BlockSpec(memory_space=pltpu.VMEM)
        smem = pl.BlockSpec(memory_space=pltpu.SMEM)
        hbm = pl.BlockSpec(memory_space=pl.ANY)
        dma = pltpu.SemaphoreType.DMA
        text_total = seq_count * TEXT_SLOT
        result = pl.pallas_call(
            functools.partial(kernel, seq_count, span, early),
            out_shape=pltpu.VMEM((images, rows, width), BF16),
            in_specs=[smem, smem] + [vmem] * 5 + [hbm] * 6,
            out_specs=vmem,
            scratch_shapes=[
                pltpu.VMEM((rows, columns), BF16),
                pltpu.VMEM((rows, columns), BF16),
                pltpu.VMEM((rows, columns), BF16),
                pltpu.VMEM((seq_count, TEXT_SLOT, LANES), BF16),
                pltpu.VMEM((seq_count, TEXT_SLOT, LANES), BF16),
                pltpu.VMEM((seq_count, half, LANES), BF16),
                pltpu.VMEM((seq_count, half, LANES), BF16),
                pltpu.VMEM((seq_count, rows, LANES), BF16),
                pltpu.VMEM((seq_count, rows, LANES), BF16),
                pltpu.VMEM((seq_count, half, LANES), BF16),
                pltpu.VMEM((seq_count, half, LANES), BF16),
                pltpu.VMEM((2, TEXT_SLOT, columns), F32),
                pltpu.VMEM((text_total, LANES), BF16),
                pltpu.VMEM((text_total, LANES), BF16),
                pltpu.VMEM((seq_count * rows, LANES), BF16),
                pltpu.VMEM((seq_count * rows, LANES), BF16),
                pltpu.VMEM((early * span * rows, LANES), F32),
                pltpu.VMEM((TEXT_SLOT, LANES), F32),
                pltpu.VMEM((TEXT_SLOT, width), F32),
                pltpu.VMEM(out_weight.shape[1:], BF16),
                pltpu.VMEM((images, rows, width), BF16),
                pltpu.VMEM((images, rows, width), F32),
                dma((4,)),
                dma,
                dma,
                dma,
                dma((blocks,)),
                dma,
                dma((blocks,)),
                dma,
                dma((blocks,)),
                dma,
                dma,
            ],
            compiler_params=pltpu.CompilerParams(
                collective_id=0, has_side_effects=True, vmem_limit_bytes=56 * 1024 * 1024
            ),
            name="joint_attention",
        )(
            text_count,
            timesteps[0],
            text_keys[0],
            text_values[0],
            query_gain,
            key_gain,
            gate_weight[0].T,
            queries[0],
            image_keys[0],
            image_values[0],
            out_weight[0],
            stale[0],
            fresh,
        )
        return result[None]

    return jax.shard_map(
        step,
        mesh=mesh,
        in_specs=(
            P("section", None, "seq", None),
            P(None, "seq", None),
            P("section", "seq", None),
            P("section", "seq", None),
            P("section", "seq", None),
            P("section", "seq", None),
            P("section", "seq", None),
            P(),
            P("section", None),
            P("section", None),
            P("section", None),
            P("section", None, None),
            P("section", None, "seq"),
        ),
        out_specs=P("section", None, "seq", None),
        check_vma=False,
    )
```

```python
import functools
import math

import jax
import jax.numpy as jnp
from jax import lax
from jax.experimental import pallas as pl
from jax.experimental.pallas import tpu as pltpu
from jax.sharding import PartitionSpec as P

MESH = pl.DeviceIdType.MESH
HD = 64
LANES = 128
TEMB = 256
TEXT_SLOT = 8
SCALE = math.log2(math.e) / math.sqrt(HD)
F32 = jnp.float32
BF16 = jnp.bfloat16


def lanes_below_half(shape):
    return lax.broadcasted_iota(jnp.int32, shape, len(shape) - 1) < HD


def swap_halves(data):
    return pltpu.roll(data, HD, len(data.shape) - 1)


def normed(parts, gain):
    data = jnp.concatenate(parts, axis=0)
    squares = data * data
    high = squares.astype(BF16)
    low = (squares - high.astype(F32)).astype(BF16)
    row = lax.broadcasted_iota(jnp.int32, (2 * LANES, LANES), 0) // HD
    col = lax.broadcasted_iota(jnp.int32, (2 * LANES, LANES), 1) // HD
    halves = jnp.where(row % 2 == col, 1.0, 0.0).astype(BF16)
    total = jnp.dot(jnp.concatenate([high, low], axis=1), halves, preferred_element_type=F32)
    data = data * lax.rsqrt(total * (1.0 / HD) + 1e-6) * gain
    sizes = [part.shape[0] for part in parts]
    return [data[sum(sizes[:at]) : sum(sizes[: at + 1])] for at in range(len(parts))]


def kernel(
    seq_count,
    span,
    early,
    counts,
    times,
    text_keys_hbm,
    text_values_hbm,
    query_gain_hbm,
    key_gain_hbm,
    gate_weight_hbm,
    queries_hbm,
    keys_hbm,
    values_hbm,
    out_weight,
    stale,
    fresh,
    out,
    text_keys,
    text_values,
    query_gain,
    key_gain,
    gate_weight,
    queries,
    keys,
    values,
    text_send,
    text_recv,
    q_send,
    q_recv,
    kv_send,
    kv_recv,
    o_send,
    o_recv,
    text_pad,
    text_k,
    text_v,
    value_aug,
    query_rows,
    total,
    gate_pad,
    gate_acc,
    weight,
    block_in,
    projected,
    load_sem,
    text_send_sem,
    text_recv_sem,
    q_send_sem,
    q_recv_sem,
    kv_send_sem,
    kv_recv_sem,
    o_send_sem,
    o_recv_sem,
    shift_send_sem,
    shift_recv_sem,
):
    me = lax.axis_index("seq")
    section = lax.axis_index("section")
    sections = lax.axis_size("section")
    rows = queries.shape[0]
    half = rows // 2
    text_rows = text_keys.shape[0]
    blocks = seq_count // span
    my_block = (me // 16) * 2 + (me % 4) // 2
    my_place = ((me // 4) % 4) * 2 + me % 2
    my_label = my_block * span + my_place
    way = 1 - 2 * (section % 2)

    def device_at(block, place):
        return (block // 2) * 16 + (place // 2) * 4 + (block % 2) * 2 + place % 2

    def tile_index(block, at):
        return (block // 2) * 8 + at * 2 + block % 2

    pairs = range(span // 2)
    turns = [2, 6, 4, 0, 3, 7, 5, 1]
    block_rows = span * rows
    gate_span = gate_weight.shape[0]
    width = out.shape[2]
    text_total = seq_count * TEXT_SLOT

    barrier = pltpu.get_barrier_semaphore()

    def greet(step, carry):
        pl.semaphore_signal(
            barrier, inc=1, device_id={"seq": lax.rem(me + step, seq_count)}, device_id_type=MESH
        )
        return carry

    lax.fori_loop(1, seq_count, greet, 0)

    @pl.when(section > 0)
    def _():
        pl.semaphore_signal(barrier, inc=1, device_id={"section": section - 1}, device_id_type=MESH)

    loads = [
        pltpu.make_async_copy(source, target, load_sem.at[at])
        for at, (source, target) in enumerate(
            (
                (queries_hbm, queries),
                (keys_hbm, keys),
                (values_hbm, values),
                (out_weight, weight),
                (text_keys_hbm, text_keys),
                (text_values_hbm, text_values),
                (query_gain_hbm, query_gain),
                (key_gain_hbm, key_gain),
                (gate_weight_hbm, gate_weight),
            )
        )
    ]
    for load in loads[4:] + loads[:4]:
        load.start()
    for load in loads[4:]:
        load.wait()

    text_pad[...] = jnp.zeros_like(text_pad)
    text_pad[0, 0:text_rows, :] = text_keys[...].astype(F32)
    text_pad[1, 0:text_rows, :] = text_values[...].astype(F32)
    query_gain_both = jnp.concatenate([query_gain[...]] * 2, axis=1)
    key_gain_both = jnp.concatenate([key_gain[...]] * 2, axis=1)

    row8 = lax.broadcasted_iota(jnp.int32, (8, LANES), 0)
    lane8 = lax.broadcasted_iota(jnp.int32, (8, LANES), 1)
    stamp = jnp.where(row8 % 2 == 0, times[0], times[1]).astype(F32)
    angles = stamp * jnp.exp(lane8.astype(F32) * (-math.log(10000.0) / (TEMB // 2)))
    features = jnp.concatenate([jnp.cos(angles), jnp.sin(angles)], axis=1)
    activated = (features / (1.0 + jnp.exp(-features))).astype(BF16)
    gate_pad[...] = jnp.zeros_like(gate_pad)
    gate_pad[:, 0:gate_span] = lax.dot_general(
        activated, gate_weight[...], (((1,), (1,)), ((), ())), preferred_element_type=F32
    )
    gate_share = gate_pad[...]
    gate_high = gate_share.astype(BF16).astype(F32)
    gate_rows = jnp.where(lane8 < HD, gate_high, swap_halves(gate_share - gate_high))

    below = lanes_below_half((rows, LANES))
    below8 = lanes_below_half((TEXT_SLOT, LANES))
    below_half = lanes_below_half((half, LANES))

    def tile(index):
        return pl.ds(pl.multiple_of(index * LANES, LANES), LANES)

    def push(send, recv, send_sem, recv_sem, target):
        pltpu.make_async_remote_copy(
            send, recv, send_sem, recv_sem, device_id={"seq": target}, device_id_type=MESH
        ).start()

    def pack_text(step, carry):
        first = step * span
        normed_keys = normed([text_pad[0, :, tile(first // 2 + at)] for at in pairs], key_gain_both)
        for at, text_key in zip(pairs, normed_keys):
            text_value = text_pad[1, :, tile(first // 2 + at)]
            one = jnp.where(below8, text_key, swap_halves(text_value))
            two = jnp.where(below8, swap_halves(text_key), text_value)
            text_send[first + 2 * at] = jnp.where(row8 < text_rows, one, gate_rows).astype(BF16)
            text_send[first + 2 * at + 1] = jnp.where(row8 < text_rows, two, gate_rows).astype(BF16)
        return carry

    lax.fori_loop(0, blocks, pack_text, 0)
    text_recv[me] = text_send[me]

    @pl.when(section < sections - 1)
    def _():
        pl.semaphore_wait(barrier, seq_count)

    @pl.when(section == sections - 1)
    def _():
        pl.semaphore_wait(barrier, seq_count - 1)

    def send_text(step, carry):
        target = lax.rem(me + step, seq_count)
        push(text_send.at[target], text_recv.at[me], text_send_sem, text_recv_sem, target)
        return carry

    lax.fori_loop(1, seq_count, send_text, 0)

    loads[0].wait()

    def pack_q(step, carry):
        block = lax.rem(my_block + step * way + blocks, blocks)
        first = block * span
        parts = normed([queries[:, tile(tile_index(block, at))].astype(F32) for at in pairs], query_gain_both)
        for at, data in zip(pairs, parts):
            data = data.astype(BF16)
            top, bottom = data[0:half], data[half:]
            q_send[first + 2 * at] = jnp.where(below_half, top, swap_halves(bottom))
            q_send[first + 2 * at + 1] = jnp.where(below_half, swap_halves(top), bottom)
        for turn in turns:
            place = lax.rem(my_place + turn * way + span, span)
            slot = step * span + turn

            @pl.when(slot > 0)
            def _(place=place, slot=slot):
                push(
                    q_send.at[first + place],
                    q_recv.at[slot],
                    q_send_sem,
                    q_recv_sem.at[step],
                    device_at(block, place),
                )

        return carry

    lax.fori_loop(0, early, pack_q, 0)
    q_recv[0] = q_send[my_label]

    loads[1].wait()
    loads[2].wait()

    def pack_kv(step, carry):
        block = lax.rem(my_block + step * way + blocks, blocks)
        first = block * span
        parts = normed([keys[:, tile(tile_index(block, at))].astype(F32) for at in pairs], key_gain_both)
        for at, key in zip(pairs, parts):
            key = key.astype(BF16)
            value = values[:, tile(tile_index(block, at))]
            kv_send[first + 2 * at] = jnp.where(below, key, swap_halves(value))
            kv_send[first + 2 * at + 1] = jnp.where(below, swap_halves(key), value)
        for turn in turns:
            place = lax.rem(my_place + turn * way + span, span)
            slot = step * span + turn

            @pl.when(slot > 0)
            def _(place=place, slot=slot):
                push(
                    kv_send.at[first + place],
                    kv_recv.at[slot],
                    kv_send_sem,
                    kv_recv_sem.at[step],
                    device_at(block, place),
                )

        return carry

    lax.fori_loop(0, blocks, pack_kv, 0)
    kv_recv[0] = kv_send[my_label]

    lax.fori_loop(early, blocks, pack_q, 0)

    @pl.when(section == 0)
    def _():
        pltpu.make_async_copy(fresh, block_in, shift_recv_sem).start()

    shift = pltpu.make_async_remote_copy(
        stale,
        block_in,
        shift_send_sem,
        shift_recv_sem,
        device_id={"section": lax.rem(section + 1, sections)},
        device_id_type=MESH,
    )

    @pl.when(section < sections - 1)
    def _():
        shift.start()

    def await_slots(recv, count, sem):
        part = recv.at[pl.ds(0, count)]
        pltpu.make_async_copy(part, part, sem).wait()

    def await_step(recv, step, sem):
        if isinstance(step, int):
            await_slots(recv, span if step else span - 1, sem.at[step])
            return

        @pl.when(step == 0)
        def _():
            await_slots(recv, span - 1, sem.at[0])

        @pl.when(step > 0)
        def _():
            await_slots(recv, span, sem.at[step])

    await_slots(text_recv, seq_count - 1, text_recv_sem)
    live_count = counts[me // (seq_count // 2)]
    text_all = text_recv[...].astype(F32).reshape(text_total, LANES)
    place = lax.broadcasted_iota(jnp.int32, (text_total, LANES), 0)
    within = place % TEXT_SLOT
    text_k[...] = jnp.where(within < text_rows, text_all, 0.0).astype(BF16)
    live = (within < text_rows) & ((place // TEXT_SLOT) * text_rows + within < live_count)
    text_v[...] = jnp.where(
        live, jnp.where(lanes_below_half((text_total, LANES)), 1.0, text_all), 0.0
    ).astype(BF16)
    gate_tiles = [jnp.zeros((TEXT_SLOT, LANES), F32) for _ in range(width // LANES)]
    for source in range(seq_count):
        at, ahead = divmod(source * gate_span, LANES)
        share = text_recv[source].astype(F32)
        share = jnp.where(below8, share + swap_halves(share), 0.0)
        if ahead > 0:
            share = pltpu.roll(share, ahead, 1)
        if ahead + gate_span > LANES:
            gate_tiles[at + 1] = gate_tiles[at + 1] + jnp.where(lane8 < ahead, share, 0.0)
            share = jnp.where(lane8 < ahead, 0.0, share)
        gate_tiles[at] = gate_tiles[at] + share
    for at, gate_tile in enumerate(gate_tiles):
        gate_acc[:, at * LANES : (at + 1) * LANES] = gate_tile

    left = lanes_below_half((block_rows // 2, LANES))

    def rows_of(block):
        start = block * block_rows
        return pl.ds(start if isinstance(start, int) else pl.multiple_of(start, block_rows), block_rows)

    def slots_of(block):
        start = block * span
        return pl.ds(start if isinstance(start, int) else pl.multiple_of(start, span), span)

    def spread(block):
        await_step(q_recv, block, q_recv_sem)
        packed = q_recv[slots_of(block)].reshape(block_rows // 2, LANES)
        zero = jnp.zeros((), BF16)
        query_rows[rows_of(block), :] = jnp.concatenate(
            [jnp.where(left, packed, zero), jnp.where(left, swap_halves(packed), zero)], axis=0
        )

    def attend(block, key, value):
        scores = lax.dot_general(
            query_rows[rows_of(block), :], key, (((1,), (1,)), ((), ())), preferred_element_type=F32
        )
        weights = jnp.exp2(scores * SCALE).astype(BF16)
        return jnp.dot(weights, value, preferred_element_type=F32)

    def keys_of(step):
        return kv_recv[slots_of(step)].reshape(block_rows, LANES)

    def prepare(step):
        await_step(kv_recv, step, kv_recv_sem)
        value_aug[rows_of(step), :] = jnp.where(
            lanes_below_half((block_rows, LANES)), jnp.ones((), BF16), keys_of(step)
        )

    def attend_step(block, step):
        return attend(block, keys_of(step), value_aug[rows_of(step), :])

    def finish(block, summed):
        result = summed / swap_halves(summed)
        top, bottom = result[0 : block_rows // 2], result[block_rows // 2 :]
        mixed = jnp.where(left, swap_halves(top), bottom).astype(BF16)
        o_send[slots_of(block)] = mixed.reshape(span, half, LANES)
        from_block = lax.rem(my_block - block * way + blocks, blocks)
        for turn in turns:
            source = device_at(from_block, lax.rem(my_place - turn * way + span, span))
            slot = block * span + turn
            if not isinstance(slot, int) or slot > 0:
                push(o_send.at[slot], o_recv.at[my_label], o_send_sem, o_recv_sem.at[block], source)

    for block in range(early):
        spread(block)
    for block in range(early):
        total[rows_of(block), :] = attend(block, text_k[...], text_v[...])

    def meet(step, carry):
        prepare(step)
        for block in range(early):
            total[rows_of(block), :] += attend_step(block, step)
        return carry

    lax.fori_loop(0, blocks - 1, meet, 0)
    prepare(blocks - 1)
    for block in range(early):
        finish(block, total[rows_of(block), :] + attend_step(block, blocks - 1))

    def attend_all(block, carry):
        spread(block)
        summed = attend(block, text_k[...], text_v[...])
        for step in range(blocks):
            summed = summed + attend_step(block, step)
        finish(block, summed)
        return carry

    lax.fori_loop(early, blocks, attend_all, 0)
    o_recv[my_label] = o_send[0]

    loads[3].wait()
    projected[...] = jnp.zeros_like(projected)
    spans = [(start, min(start + 512, width)) for start in range(0, width, 512)]

    def heads_of(step):
        block = lax.rem(my_block + step * way + blocks, blocks)
        return block, block // (blocks // 2)

    def arrived(step, block):
        await_step(o_recv, step, o_recv_sem)
        tops, bottoms = [], []
        for at in pairs:
            one, two = o_recv[block * span + 2 * at], o_recv[block * span + 2 * at + 1]
            tops.append(jnp.where(below_half, one, swap_halves(two)))
            bottoms.append(jnp.where(below_half, swap_halves(one), two))
        return jnp.concatenate(
            [jnp.concatenate(tops, axis=1), jnp.concatenate(bottoms, axis=1)], axis=0
        )

    def product(attended, block, start, stop):
        weight_tiles = [tile(lax.rem(tile_index(block, at), seq_count // 4)) for at in pairs]
        part = jnp.concatenate([weight[part_rows, start:stop] for part_rows in weight_tiles], axis=0)
        return jnp.dot(attended, part, preferred_element_type=F32)

    def project(step, carry):
        block, image = heads_of(step)
        attended = arrived(step, block)
        for start, stop in spans:
            projected[image, :, start:stop] += product(attended, block, start, stop)
        return carry

    lax.fori_loop(0, blocks - 1, project, 0)

    @pl.when(section == 0)
    def _():
        pltpu.make_async_copy(fresh, block_in, shift_recv_sem).wait()

    @pl.when(section > 0)
    def _():
        shift.wait_recv()

    def mix(image, start, stop, summed):
        gate = gate_acc[pl.ds(text_rows + image, 1), start:stop]
        held = block_in[image, :, start:stop].astype(F32)
        out[image, :, start:stop] = (held + gate * summed).astype(BF16)

    block, image = heads_of(blocks - 1)
    for start, stop in spans:
        mix(1 - image, start, stop, projected[1 - image, :, start:stop])
    attended = arrived(blocks - 1, block)
    for start, stop in spans:
        mix(image, start, stop, projected[image, :, start:stop] + product(attended, block, start, stop))

    for send, sem in (
        (text_send, text_send_sem),
        (q_send, q_send_sem),
        (kv_send, kv_send_sem),
        (o_send, o_send_sem),
    ):
        await_slots(send, seq_count - 1, sem)

    @pl.when(section < sections - 1)
    def _():
        shift.wait_send()


def solution(mesh):
    seq_count = mesh.shape["seq"]
    span = 8
    early = 6

    def step(
        stale,
        fresh,
        queries,
        image_keys,
        image_values,
        text_keys,
        text_values,
        text_count,
        timesteps,
        query_gain,
        key_gain,
        out_weight,
        gate_weight,
    ):
        images, rows, width = fresh.shape
        half = rows // 2
        columns = queries.shape[2]
        blocks = seq_count // span
        vmem = pl.BlockSpec(memory_space=pltpu.VMEM)
        smem = pl.BlockSpec(memory_space=pltpu.SMEM)
        hbm = pl.BlockSpec(memory_space=pl.ANY)
        dma = pltpu.SemaphoreType.DMA
        text_total = seq_count * TEXT_SLOT
        result = pl.pallas_call(
            functools.partial(kernel, seq_count, span, early),
            out_shape=pltpu.VMEM((images, rows, width), BF16),
            in_specs=[smem, smem] + [hbm] * 11,
            out_specs=vmem,
            scratch_shapes=[
                pltpu.VMEM(text_keys.shape[1:], BF16),
                pltpu.VMEM(text_values.shape[1:], BF16),
                pltpu.VMEM(query_gain.shape, F32),
                pltpu.VMEM(key_gain.shape, F32),
                pltpu.VMEM(gate_weight.shape[:0:-1], BF16),
                pltpu.VMEM((rows, columns), BF16),
                pltpu.VMEM((rows, columns), BF16),
                pltpu.VMEM((rows, columns), BF16),
                pltpu.VMEM((seq_count, TEXT_SLOT, LANES), BF16),
                pltpu.VMEM((seq_count, TEXT_SLOT, LANES), BF16),
                pltpu.VMEM((seq_count, half, LANES), BF16),
                pltpu.VMEM((seq_count, half, LANES), BF16),
                pltpu.VMEM((seq_count, rows, LANES), BF16),
                pltpu.VMEM((seq_count, rows, LANES), BF16),
                pltpu.VMEM((seq_count, half, LANES), BF16),
                pltpu.VMEM((seq_count, half, LANES), BF16),
                pltpu.VMEM((2, TEXT_SLOT, columns), F32),
                pltpu.VMEM((text_total, LANES), BF16),
                pltpu.VMEM((text_total, LANES), BF16),
                pltpu.VMEM((seq_count * rows, LANES), BF16),
                pltpu.VMEM((seq_count * rows, LANES), BF16),
                pltpu.VMEM((early * span * rows, LANES), F32),
                pltpu.VMEM((TEXT_SLOT, LANES), F32),
                pltpu.VMEM((TEXT_SLOT, width), F32),
                pltpu.VMEM(out_weight.shape[1:], BF16),
                pltpu.VMEM((images, rows, width), BF16),
                pltpu.VMEM((images, rows, width), F32),
                dma((9,)),
                dma,
                dma,
                dma,
                dma((blocks,)),
                dma,
                dma((blocks,)),
                dma,
                dma((blocks,)),
                dma,
                dma,
            ],
            compiler_params=pltpu.CompilerParams(
                collective_id=0, has_side_effects=True, vmem_limit_bytes=56 * 1024 * 1024
            ),
            name="joint_attention",
        )(
            text_count,
            timesteps[0],
            text_keys[0],
            text_values[0],
            query_gain,
            key_gain,
            gate_weight[0].T,
            queries[0],
            image_keys[0],
            image_values[0],
            out_weight[0],
            stale[0],
            fresh,
        )
        return result[None]

    return jax.shard_map(
        step,
        mesh=mesh,
        in_specs=(
            P("section", None, "seq", None),
            P(None, "seq", None),
            P("section", "seq", None),
            P("section", "seq", None),
            P("section", "seq", None),
            P("section", "seq", None),
            P("section", "seq", None),
            P(),
            P("section", None),
            P("section", None),
            P("section", None),
            P("section", None, None),
            P("section", None, "seq"),
        ),
        out_specs=P("section", None, "seq", None),
        check_vma=False,
    )
```

```python
import functools
import math

import jax
import jax.numpy as jnp
from jax import lax
from jax.experimental import pallas as pl
from jax.experimental.pallas import tpu as pltpu
from jax.sharding import PartitionSpec as P

MESH = pl.DeviceIdType.MESH
HD = 64
LANES = 128
TEMB = 256
TEXT_SLOT = 8
SCALE = math.log2(math.e) / math.sqrt(HD)
F32 = jnp.float32
BF16 = jnp.bfloat16


def lanes_below_half(shape):
    return lax.broadcasted_iota(jnp.int32, shape, len(shape) - 1) < HD


def swap_halves(data):
    return pltpu.roll(data, HD, len(data.shape) - 1)


def normed(parts, gain):
    data = jnp.concatenate(parts, axis=0)
    squares = data * data
    high = squares.astype(BF16)
    low = (squares - high.astype(F32)).astype(BF16)
    row = lax.broadcasted_iota(jnp.int32, (2 * LANES, LANES), 0) // HD
    col = lax.broadcasted_iota(jnp.int32, (2 * LANES, LANES), 1) // HD
    halves = jnp.where(row % 2 == col, 1.0, 0.0).astype(BF16)
    total = jnp.dot(jnp.concatenate([high, low], axis=1), halves, preferred_element_type=F32)
    data = data * lax.rsqrt(total * (1.0 / HD) + 1e-6) * gain
    sizes = [part.shape[0] for part in parts]
    return [data[sum(sizes[:at]) : sum(sizes[: at + 1])] for at in range(len(parts))]


def kernel(
    seq_count,
    span,
    early,
    counts,
    times,
    text_keys_hbm,
    text_values_hbm,
    query_gain_hbm,
    key_gain_hbm,
    gate_weight_hbm,
    queries_hbm,
    keys_hbm,
    values_hbm,
    out_weight,
    stale,
    fresh,
    out,
    text_keys,
    text_values,
    query_gain,
    key_gain,
    gate_weight,
    queries,
    keys,
    values,
    text_send,
    text_recv,
    q_send,
    q_recv,
    kv_send,
    kv_recv,
    o_send,
    o_recv,
    text_pad,
    text_k,
    text_v,
    value_aug,
    query_rows,
    total,
    gate_pad,
    gate_acc,
    weight,
    block_in,
    projected,
    load_sem,
    text_send_sem,
    text_recv_sem,
    q_send_sem,
    q_recv_sem,
    kv_send_sem,
    kv_recv_sem,
    o_send_sem,
    o_recv_sem,
    shift_send_sem,
    shift_recv_sem,
):
    me = lax.axis_index("seq")
    section = lax.axis_index("section")
    sections = lax.axis_size("section")
    rows = queries.shape[0]
    half = rows // 2
    text_rows = text_keys.shape[0]
    blocks = seq_count // span
    my_block = (me // 16) * 2 + (me % 4) // 2
    my_place = ((me // 4) % 4) * 2 + me % 2
    my_label = my_block * span + my_place
    way = 1 - 2 * (section % 2)

    def device_at(block, place):
        return (block // 2) * 16 + (place // 2) * 4 + (block % 2) * 2 + place % 2

    def tile_index(block, at):
        return (block // 2) * 8 + at * 2 + block % 2

    pairs = range(span // 2)
    turns = [2, 6, 4, 0, 3, 7, 5, 1]
    block_rows = span * rows
    gate_span = gate_weight.shape[0]
    width = out.shape[2]
    text_total = seq_count * TEXT_SLOT

    barrier = pltpu.get_barrier_semaphore()

    def greet(step, carry):
        pl.semaphore_signal(
            barrier, inc=1, device_id={"seq": lax.rem(me + step, seq_count)}, device_id_type=MESH
        )
        return carry

    lax.fori_loop(1, seq_count, greet, 0)

    @pl.when(section > 0)
    def _():
        pl.semaphore_signal(barrier, inc=1, device_id={"section": section - 1}, device_id_type=MESH)

    loads = [
        pltpu.make_async_copy(source, target, load_sem.at[at])
        for at, (source, target) in enumerate(
            (
                (queries_hbm, queries),
                (keys_hbm, keys),
                (values_hbm, values),
                (out_weight, weight),
                (text_keys_hbm, text_keys),
                (text_values_hbm, text_values),
                (query_gain_hbm, query_gain),
                (key_gain_hbm, key_gain),
                (gate_weight_hbm, gate_weight),
            )
        )
    ]
    for load in loads[4:] + loads[:4]:
        load.start()
    for load in loads[4:]:
        load.wait()

    text_pad[...] = jnp.zeros_like(text_pad)
    text_pad[0, 0:text_rows, :] = text_keys[...].astype(F32)
    text_pad[1, 0:text_rows, :] = text_values[...].astype(F32)
    query_gain_both = jnp.concatenate([query_gain[...]] * 2, axis=1)
    key_gain_both = jnp.concatenate([key_gain[...]] * 2, axis=1)

    row8 = lax.broadcasted_iota(jnp.int32, (8, LANES), 0)
    lane8 = lax.broadcasted_iota(jnp.int32, (8, LANES), 1)
    stamp = jnp.where(row8 % 2 == 0, times[0], times[1]).astype(F32)
    angles = stamp * jnp.exp(lane8.astype(F32) * (-math.log(10000.0) / (TEMB // 2)))
    features = jnp.concatenate([jnp.cos(angles), jnp.sin(angles)], axis=1)
    activated = (features / (1.0 + jnp.exp(-features))).astype(BF16)
    gate_pad[...] = jnp.zeros_like(gate_pad)
    gate_pad[:, 0:gate_span] = lax.dot_general(
        activated, gate_weight[...], (((1,), (1,)), ((), ())), preferred_element_type=F32
    )
    gate_share = gate_pad[...]
    gate_high = gate_share.astype(BF16).astype(F32)
    gate_rows = jnp.where(lane8 < HD, gate_high, swap_halves(gate_share - gate_high))

    below = lanes_below_half((rows, LANES))
    below8 = lanes_below_half((TEXT_SLOT, LANES))
    below_half = lanes_below_half((half, LANES))

    def tile(index):
        return pl.ds(pl.multiple_of(index * LANES, LANES), LANES)

    def push(send, recv, send_sem, recv_sem, target):
        pltpu.make_async_remote_copy(
            send, recv, send_sem, recv_sem, device_id={"seq": target}, device_id_type=MESH
        ).start()

    loads[0].wait()

    def pack_q(step, carry):
        block = lax.rem(my_block + step * way + blocks, blocks)
        first = block * span
        parts = normed([queries[:, tile(tile_index(block, at))].astype(F32) for at in pairs], query_gain_both)
        for at, data in zip(pairs, parts):
            data = data.astype(BF16)
            top, bottom = data[0:half], data[half:]
            q_send[first + 2 * at] = jnp.where(below_half, top, swap_halves(bottom))
            q_send[first + 2 * at + 1] = jnp.where(below_half, swap_halves(top), bottom)
        return carry

    lax.fori_loop(0, blocks, pack_q, 0)
    q_recv[0] = q_send[my_label]

    @pl.when(section < sections - 1)
    def _():
        pl.semaphore_wait(barrier, seq_count)

    @pl.when(section == sections - 1)
    def _():
        pl.semaphore_wait(barrier, seq_count - 1)

    def send_q(step, carry):
        block = lax.rem(my_block + step * way + blocks, blocks)
        first = block * span
        for turn in turns:
            place = lax.rem(my_place + turn * way + span, span)
            slot = step * span + turn

            @pl.when(slot > 0)
            def _(place=place, slot=slot):
                push(
                    q_send.at[first + place],
                    q_recv.at[slot],
                    q_send_sem,
                    q_recv_sem.at[step],
                    device_at(block, place),
                )

        return carry

    lax.fori_loop(0, early, send_q, 0)

    def pack_text(step, carry):
        first = step * span
        normed_keys = normed([text_pad[0, :, tile(first // 2 + at)] for at in pairs], key_gain_both)
        for at, text_key in zip(pairs, normed_keys):
            text_value = text_pad[1, :, tile(first // 2 + at)]
            one = jnp.where(below8, text_key, swap_halves(text_value))
            two = jnp.where(below8, swap_halves(text_key), text_value)
            text_send[first + 2 * at] = jnp.where(row8 < text_rows, one, gate_rows).astype(BF16)
            text_send[first + 2 * at + 1] = jnp.where(row8 < text_rows, two, gate_rows).astype(BF16)
        return carry

    lax.fori_loop(0, blocks, pack_text, 0)
    text_recv[me] = text_send[me]

    def send_text(step, carry):
        target = lax.rem(me + step, seq_count)
        push(text_send.at[target], text_recv.at[me], text_send_sem, text_recv_sem, target)
        return carry

    lax.fori_loop(1, seq_count, send_text, 0)

    loads[1].wait()
    loads[2].wait()

    def pack_kv(step, carry):
        block = lax.rem(my_block + step * way + blocks, blocks)
        first = block * span
        parts = normed([keys[:, tile(tile_index(block, at))].astype(F32) for at in pairs], key_gain_both)
        for at, key in zip(pairs, parts):
            key = key.astype(BF16)
            value = values[:, tile(tile_index(block, at))]
            kv_send[first + 2 * at] = jnp.where(below, key, swap_halves(value))
            kv_send[first + 2 * at + 1] = jnp.where(below, swap_halves(key), value)
        for turn in turns:
            place = lax.rem(my_place + turn * way + span, span)
            slot = step * span + turn

            @pl.when(slot > 0)
            def _(place=place, slot=slot):
                push(
                    kv_send.at[first + place],
                    kv_recv.at[slot],
                    kv_send_sem,
                    kv_recv_sem.at[step],
                    device_at(block, place),
                )

        return carry

    lax.fori_loop(0, blocks, pack_kv, 0)
    kv_recv[0] = kv_send[my_label]

    lax.fori_loop(early, blocks, send_q, 0)

    @pl.when(section == 0)
    def _():
        pltpu.make_async_copy(fresh, block_in, shift_recv_sem).start()

    shift = pltpu.make_async_remote_copy(
        stale,
        block_in,
        shift_send_sem,
        shift_recv_sem,
        device_id={"section": lax.rem(section + 1, sections)},
        device_id_type=MESH,
    )

    @pl.when(section < sections - 1)
    def _():
        shift.start()

    def await_slots(recv, count, sem):
        part = recv.at[pl.ds(0, count)]
        pltpu.make_async_copy(part, part, sem).wait()

    def await_step(recv, step, sem):
        if isinstance(step, int):
            await_slots(recv, span if step else span - 1, sem.at[step])
            return

        @pl.when(step == 0)
        def _():
            await_slots(recv, span - 1, sem.at[0])

        @pl.when(step > 0)
        def _():
            await_slots(recv, span, sem.at[step])

    await_slots(text_recv, seq_count - 1, text_recv_sem)
    live_count = counts[me // (seq_count // 2)]
    text_all = text_recv[...].astype(F32).reshape(text_total, LANES)
    place = lax.broadcasted_iota(jnp.int32, (text_total, LANES), 0)
    within = place % TEXT_SLOT
    text_k[...] = jnp.where(within < text_rows, text_all, 0.0).astype(BF16)
    live = (within < text_rows) & ((place // TEXT_SLOT) * text_rows + within < live_count)
    text_v[...] = jnp.where(
        live, jnp.where(lanes_below_half((text_total, LANES)), 1.0, text_all), 0.0
    ).astype(BF16)
    gate_tiles = [jnp.zeros((TEXT_SLOT, LANES), F32) for _ in range(width // LANES)]
    for source in range(seq_count):
        at, ahead = divmod(source * gate_span, LANES)
        share = text_recv[source].astype(F32)
        share = jnp.where(below8, share + swap_halves(share), 0.0)
        if ahead > 0:
            share = pltpu.roll(share, ahead, 1)
        if ahead + gate_span > LANES:
            gate_tiles[at + 1] = gate_tiles[at + 1] + jnp.where(lane8 < ahead, share, 0.0)
            share = jnp.where(lane8 < ahead, 0.0, share)
        gate_tiles[at] = gate_tiles[at] + share
    for at, gate_tile in enumerate(gate_tiles):
        gate_acc[:, at * LANES : (at + 1) * LANES] = gate_tile

    left = lanes_below_half((block_rows // 2, LANES))

    def rows_of(block):
        start = block * block_rows
        return pl.ds(start if isinstance(start, int) else pl.multiple_of(start, block_rows), block_rows)

    def slots_of(block):
        start = block * span
        return pl.ds(start if isinstance(start, int) else pl.multiple_of(start, span), span)

    def spread(block):
        await_step(q_recv, block, q_recv_sem)
        packed = q_recv[slots_of(block)].reshape(block_rows // 2, LANES)
        zero = jnp.zeros((), BF16)
        query_rows[rows_of(block), :] = jnp.concatenate(
            [jnp.where(left, packed, zero), jnp.where(left, swap_halves(packed), zero)], axis=0
        )

    def attend(block, key, value):
        scores = lax.dot_general(
            query_rows[rows_of(block), :], key, (((1,), (1,)), ((), ())), preferred_element_type=F32
        )
        weights = jnp.exp2(scores * SCALE).astype(BF16)
        return jnp.dot(weights, value, preferred_element_type=F32)

    def keys_of(step):
        return kv_recv[slots_of(step)].reshape(block_rows, LANES)

    def prepare(step):
        await_step(kv_recv, step, kv_recv_sem)
        value_aug[rows_of(step), :] = jnp.where(
            lanes_below_half((block_rows, LANES)), jnp.ones((), BF16), keys_of(step)
        )

    def attend_step(block, step):
        return attend(block, keys_of(step), value_aug[rows_of(step), :])

    def finish(block, summed):
        result = summed / swap_halves(summed)
        top, bottom = result[0 : block_rows // 2], result[block_rows // 2 :]
        mixed = jnp.where(left, swap_halves(top), bottom).astype(BF16)
        o_send[slots_of(block)] = mixed.reshape(span, half, LANES)
        from_block = lax.rem(my_block - block * way + blocks, blocks)
        for turn in turns:
            source = device_at(from_block, lax.rem(my_place - turn * way + span, span))
            slot = block * span + turn
            if not isinstance(slot, int) or slot > 0:
                push(o_send.at[slot], o_recv.at[my_label], o_send_sem, o_recv_sem.at[block], source)

    for block in range(early):
        spread(block)
    for block in range(early):
        total[rows_of(block), :] = attend(block, text_k[...], text_v[...])

    def meet(step, carry):
        prepare(step)
        for block in range(early):
            total[rows_of(block), :] += attend_step(block, step)
        return carry

    lax.fori_loop(0, blocks - 1, meet, 0)
    prepare(blocks - 1)
    for block in range(early):
        finish(block, total[rows_of(block), :] + attend_step(block, blocks - 1))

    def attend_all(block, carry):
        spread(block)
        summed = attend(block, text_k[...], text_v[...])
        for step in range(blocks):
            summed = summed + attend_step(block, step)
        finish(block, summed)
        return carry

    lax.fori_loop(early, blocks, attend_all, 0)
    o_recv[my_label] = o_send[0]

    loads[3].wait()
    projected[...] = jnp.zeros_like(projected)
    spans = [(start, min(start + 512, width)) for start in range(0, width, 512)]

    def heads_of(step):
        block = lax.rem(my_block + step * way + blocks, blocks)
        return block, block // (blocks // 2)

    def arrived(step, block):
        await_step(o_recv, step, o_recv_sem)
        tops, bottoms = [], []
        for at in pairs:
            one, two = o_recv[block * span + 2 * at], o_recv[block * span + 2 * at + 1]
            tops.append(jnp.where(below_half, one, swap_halves(two)))
            bottoms.append(jnp.where(below_half, swap_halves(one), two))
        return jnp.concatenate(
            [jnp.concatenate(tops, axis=1), jnp.concatenate(bottoms, axis=1)], axis=0
        )

    def product(attended, block, start, stop):
        weight_tiles = [tile(lax.rem(tile_index(block, at), seq_count // 4)) for at in pairs]
        part = jnp.concatenate([weight[part_rows, start:stop] for part_rows in weight_tiles], axis=0)
        return jnp.dot(attended, part, preferred_element_type=F32)

    def project(step, carry):
        block, image = heads_of(step)
        attended = arrived(step, block)
        for start, stop in spans:
            projected[image, :, start:stop] += product(attended, block, start, stop)
        return carry

    lax.fori_loop(0, blocks - 1, project, 0)

    @pl.when(section == 0)
    def _():
        pltpu.make_async_copy(fresh, block_in, shift_recv_sem).wait()

    @pl.when(section > 0)
    def _():
        shift.wait_recv()

    def mix(image, start, stop, summed):
        gate = gate_acc[pl.ds(text_rows + image, 1), start:stop]
        held = block_in[image, :, start:stop].astype(F32)
        out[image, :, start:stop] = (held + gate * summed).astype(BF16)

    block, image = heads_of(blocks - 1)
    for start, stop in spans:
        mix(1 - image, start, stop, projected[1 - image, :, start:stop])
    attended = arrived(blocks - 1, block)
    for start, stop in spans:
        mix(image, start, stop, projected[image, :, start:stop] + product(attended, block, start, stop))

    for send, sem in (
        (text_send, text_send_sem),
        (q_send, q_send_sem),
        (kv_send, kv_send_sem),
        (o_send, o_send_sem),
    ):
        await_slots(send, seq_count - 1, sem)

    @pl.when(section < sections - 1)
    def _():
        shift.wait_send()


def solution(mesh):
    seq_count = mesh.shape["seq"]
    span = 8
    early = 7

    def step(
        stale,
        fresh,
        queries,
        image_keys,
        image_values,
        text_keys,
        text_values,
        text_count,
        timesteps,
        query_gain,
        key_gain,
        out_weight,
        gate_weight,
    ):
        images, rows, width = fresh.shape
        half = rows // 2
        columns = queries.shape[2]
        blocks = seq_count // span
        vmem = pl.BlockSpec(memory_space=pltpu.VMEM)
        smem = pl.BlockSpec(memory_space=pltpu.SMEM)
        hbm = pl.BlockSpec(memory_space=pl.ANY)
        dma = pltpu.SemaphoreType.DMA
        text_total = seq_count * TEXT_SLOT
        result = pl.pallas_call(
            functools.partial(kernel, seq_count, span, early),
            out_shape=pltpu.VMEM((images, rows, width), BF16),
            in_specs=[smem, smem] + [hbm] * 11,
            out_specs=vmem,
            scratch_shapes=[
                pltpu.VMEM(text_keys.shape[1:], BF16),
                pltpu.VMEM(text_values.shape[1:], BF16),
                pltpu.VMEM(query_gain.shape, F32),
                pltpu.VMEM(key_gain.shape, F32),
                pltpu.VMEM(gate_weight.shape[:0:-1], BF16),
                pltpu.VMEM((rows, columns), BF16),
                pltpu.VMEM((rows, columns), BF16),
                pltpu.VMEM((rows, columns), BF16),
                pltpu.VMEM((seq_count, TEXT_SLOT, LANES), BF16),
                pltpu.VMEM((seq_count, TEXT_SLOT, LANES), BF16),
                pltpu.VMEM((seq_count, half, LANES), BF16),
                pltpu.VMEM((seq_count, half, LANES), BF16),
                pltpu.VMEM((seq_count, rows, LANES), BF16),
                pltpu.VMEM((seq_count, rows, LANES), BF16),
                pltpu.VMEM((seq_count, half, LANES), BF16),
                pltpu.VMEM((seq_count, half, LANES), BF16),
                pltpu.VMEM((2, TEXT_SLOT, columns), F32),
                pltpu.VMEM((text_total, LANES), BF16),
                pltpu.VMEM((text_total, LANES), BF16),
                pltpu.VMEM((seq_count * rows, LANES), BF16),
                pltpu.VMEM((seq_count * rows, LANES), BF16),
                pltpu.VMEM((early * span * rows, LANES), F32),
                pltpu.VMEM((TEXT_SLOT, LANES), F32),
                pltpu.VMEM((TEXT_SLOT, width), F32),
                pltpu.VMEM(out_weight.shape[1:], BF16),
                pltpu.VMEM((images, rows, width), BF16),
                pltpu.VMEM((images, rows, width), F32),
                dma((9,)),
                dma,
                dma,
                dma,
                dma((blocks,)),
                dma,
                dma((blocks,)),
                dma,
                dma((blocks,)),
                dma,
                dma,
            ],
            compiler_params=pltpu.CompilerParams(
                collective_id=0, has_side_effects=True, vmem_limit_bytes=56 * 1024 * 1024
            ),
            name="joint_attention",
        )(
            text_count,
            timesteps[0],
            text_keys[0],
            text_values[0],
            query_gain,
            key_gain,
            gate_weight[0].T,
            queries[0],
            image_keys[0],
            image_values[0],
            out_weight[0],
            stale[0],
            fresh,
        )
        return result[None]

    return jax.shard_map(
        step,
        mesh=mesh,
        in_specs=(
            P("section", None, "seq", None),
            P(None, "seq", None),
            P("section", "seq", None),
            P("section", "seq", None),
            P("section", "seq", None),
            P("section", "seq", None),
            P("section", "seq", None),
            P(),
            P("section", None),
            P("section", None),
            P("section", None),
            P("section", None, None),
            P("section", None, "seq"),
        ),
        out_specs=P("section", None, "seq", None),
        check_vma=False,
    )
```
